32 devices in a mesh: rep: 2 (over y), expert: 8 (over z, x), group: 2 (over core).
Axes of the slice: x: 2, y: 2, z: 4, core: 2. Of those that a mesh axis runs over, the one named last changes fastest.
Arguments:
- tokens: bfloat16 [4096, 1024], P(('rep', 'expert', 'group')), parts along dimension 0, may hold values from -6 to 6
- w_gate: bfloat16 [16, 1024, 384], P('expert', 'group'), may hold values from -0.1875 to 0.1875
- w_up: bfloat16 [16, 1024, 384], P('expert', 'group'), may hold values from -0.1875 to 0.1875
- w_down: bfloat16 [16, 384, 1024], P('expert', 'group'), may hold values from -0.45927933 to 0.45927933
- route_ids: int32 [4096, 8], P(('rep', 'expert', 'group')), parts along dimension 0, may hold values from 0 to 15, all different within a row; in each aligned block of 128 rows (0 to 127, 128 to 255, ...) at most 80 rows name the same one
- route_scores: float32 [4096, 8], P(('rep', 'expert', 'group')), parts along dimension 0, may hold values from 0.05 to 1
- norm_gain: float32 [1024], replicated, may hold values from 0.5 to 1.5
- class_head: bfloat16 [1024, 2000], P(None, 'expert'), may hold values from -0.59765625 to 0.59765625
- targets: int32 [16, 2, 2000], P('rep', 'group', 'expert'), parts along dimension 0, may hold values 0 or 1
Outputs:
- token_grad: bfloat16 [4096, 1024], P(('rep', 'expert', 'group')), parts along dimension 0
- head_grad: float32 [2048, 2000], P('rep', 'expert'), parts along dimension 0
The draws below stay inside these ranges and needn't reach their ends.
There are 2 independent parts, one for each index of `rep`. The reference program is written for one: setup_inputs(seed, part) draws one part's arguments, and reference() takes and returns one part's arrays. A program takes and returns all parts, laid end to end along the dimension named above; an argument that names none is the same for every part. Nothing has to cross between parts.
Inputs may be any that keep to these rules, and one draw needn't show every extreme that they name: `route_ids`: each row names 8 different experts; among the 128 tokens of one sequence no expert is named by more than 80 tokens, and in some sequences one expert is named by exactly 80.
All inputs are finite; a program needn't handle non-finite values. No bound on the sum of `targets` on one device may be relied on, other than what follows from the above.
Results may differ from the reference program's by a relative error of at most 0.022.
Values may be sent and summed in bfloat16 or wider, within the bound.
A program may use at most 64 MiB of HBM per device.

```python
import math
import jax
import jax.numpy as jnp
import numpy as np
from jax import lax

D = 1024
FF = 384
TOP = 8
LABELS = 2000
TOK_DEV = 128
EXPERTS = 16
SEQS = 16
TOKENS = 2048
CAP = 80
N_EXPERT = 8
N_GROUP = 2


def draw_tokens(key, part):
    shared = jnp.clip(jax.random.normal(jax.random.fold_in(key, 11), (SEQS, 1, D), jnp.float32), -3.0, 3.0)
    noise = jnp.clip(jax.random.normal(jax.random.fold_in(key, 12), (SEQS, TOK_DEV, D), jnp.float32), -3.0, 3.0)
    values = jnp.clip(1.5 * shared + noise, -6.0, 6.0)
    return values.reshape(TOKENS, D).astype(jnp.bfloat16)


def mixed_weight(key, salt, rows, cols, scale):
    common = jnp.clip(jax.random.normal(jax.random.fold_in(key, salt), (1, rows, cols), jnp.float32), -4.0, 4.0)
    own = jnp.clip(jax.random.normal(jax.random.fold_in(key, salt + 1), (EXPERTS, rows, cols), jnp.float32), -4.0, 4.0)
    limit = 6.0 * scale * rows ** (-0.5)
    values = (0.9 * common + 0.45 * own) * (scale * rows ** (-0.5))
    return jnp.clip(values, -limit, limit).astype(jnp.bfloat16)


def draw_w_gate(key, part):
    return mixed_weight(key, 101, D, FF, 1.0)


def draw_w_up(key, part):
    return mixed_weight(key, 201, D, FF, 1.0)


def draw_w_down(key, part):
    return mixed_weight(key, 301, FF, D, 1.5)


def place_ends(result, rng, least, high):
    shape = result.shape
    index_at = [jax.random.randint(jax.random.fold_in(rng, axis), (), 0, shape[axis]) for axis in range(len(shape))]
    result = result.at[tuple(index_at)].set(least)
    longest = shape.index(max(shape))
    index_at[longest] = (index_at[longest] + 1) % shape[longest]
    return result.at[tuple(index_at)].set(high)


def level_of(own_key, shape, cuts, smallest, top_value):
    def one(dim, blocks):
        steps = jax.random.uniform(jax.random.fold_in(jax.random.fold_in(own_key, 6), dim), (blocks,), jnp.float32, smallest / len(cuts), top_value / len(cuts))
        return jnp.repeat(jnp.exp(steps), shape[dim] // blocks).reshape((-1,) + (1,) * (len(shape) - dim - 1))

    gain = one(*cuts[0])
    for cut in cuts[1:]:
        gain = gain * one(*cut)
    return gain


def shared_out(own_key, own, number, rows, amount, top, most, lean):
    ranking = jax.random.permutation(own_key, amount)
    heavy_load, ordinary = shares(amount, rows * top, most, lean, True), shares(amount, rows * top, most, lean, False)
    places = jnp.arange(amount)

    def named(tallies, rotation):
        used = int((tallies > 0).sum())
        fixed = max(1, used // 4)
        passed = fixed + (places - fixed + rotation * (used - fixed)) % max(1, amount - fixed)
        return jnp.zeros((amount,), jnp.int32).at[ranking[jnp.where(places < fixed, places, passed)]].set(jnp.asarray(tallies, jnp.int32))

    tallies = jnp.where(number % 4 == 0, named(heavy_load, number // 4), named(ordinary, number - number // 4 - 1))
    mixed = jax.random.permutation(jax.random.fold_in(own, 3), amount)
    source_of, sink = mixed[0:amount // 2 * 2:2], mixed[1:amount // 2 * 2:2]
    room = jnp.minimum(tallies[source_of] - 1, most - tallies[sink]) // 2
    room = jnp.where((source_of == ranking[0]) | (sink == ranking[0]) | (tallies[sink] == 0), 0, jnp.maximum(room, 0))
    passed = jax.random.randint(jax.random.fold_in(own, 4), (amount // 2,), 0, 1 << 20) % (room + 1)
    tallies = tallies.at[source_of].add(-passed).at[sink].add(passed)
    members = jnp.searchsorted(jnp.cumsum(tallies), jnp.arange(rows * top), side="right").astype(jnp.int32)
    grid = members.reshape(top, rows).T
    grid = grid[jax.random.permutation(jax.random.fold_in(own, 1), rows)]
    rotation = jax.random.randint(jax.random.fold_in(own, 2), (rows, 1), 0, top)
    return jnp.take_along_axis(grid, (jnp.arange(top)[None, :] + rotation) % top, axis=1)


def shares(count, total, most, skew, full):
    weights = [(1 << 20) // math.isqrt(standing ** skew) + 1 for standing in range(1, count + 1)]
    largest = most if full else min(most, max(-(-total // count), total * weights[0] // sum(weights)))
    least = 1 if total - largest >= count - 1 else 0
    holding, rest = [largest] + [least] * (count - 1), total - largest - least * (count - 1)
    while rest > 0:
        free = [i for i in range(1, count) if holding[i] < largest] or [i for i in range(1, count) if holding[i] < most]
        mass, budget = sum([weights[i] for i in free]), rest
        for i in free:
            extra = min(most - holding[i], max(1, budget * weights[i] // mass), rest)
            holding[i] = holding[i] + extra
            rest = rest - extra
    return np.array(holding)


def centred(stream_key, dims, spread, bound, split=(), held_as=jnp.bfloat16):
    drawn = spread * jax.random.normal(stream_key, dims, jnp.float32)
    if split:
        drawn = drawn * level_of(stream_key, dims, split, -0.22, 0.18)
    return jnp.clip(drawn, -bound, bound).astype(held_as)


def setup_inputs(seed: int = 0, part: int = 0) -> dict:
    key_list = jax.random.split(jax.random.key(seed), 10)
    own_keys = jax.random.split(jax.random.fold_in(key_list[9], part), 10)
    tokens = draw_tokens(jax.random.fold_in(jax.random.fold_in(key_list[9], part), 71), part)
    w_gate = draw_w_gate(jax.random.fold_in(key_list[9], 71), part)
    w_up = draw_w_up(jax.random.fold_in(key_list[9], 71), part)
    w_down = draw_w_down(jax.random.fold_in(key_list[9], 71), part)
    route_ids_keys = jax.random.split(jax.random.fold_in(own_keys[4], 1), TOKENS // TOK_DEV)
    route_ids_turns = jax.random.permutation(jax.random.fold_in(own_keys[4], 3), TOKENS // TOK_DEV)
    route_ids = jax.vmap(lambda own, number: shared_out(jax.random.fold_in(own_keys[4], 2), own, number, TOK_DEV, EXPERTS, TOP, CAP, 2))(route_ids_keys, route_ids_turns).reshape((TOKENS, TOP))
    route_scores = jnp.clip(jnp.exp(math.log(1.0) - 2.9957323 * jax.random.uniform(own_keys[5], (TOKENS, TOP), jnp.float32) ** level_of(own_keys[5], (TOKENS, TOP), ((0, 16),), -0.2, 0.2)), 0.05, 1.0)
    norm_gain = jnp.clip(1.0 + 0.1 * jax.random.normal(key_list[6], (D,), jnp.float32), 0.5, 1.5)
    class_head = centred(key_list[7], (D, LABELS), 0.1, 0.59765625, ((1, 8),))
    targets = place_ends((jax.random.randint(own_keys[8], (N_EXPERT, N_GROUP, LABELS), 0, 8) < 1).astype(jnp.int32), jax.random.fold_in(own_keys[8], 1), 0, 1)
    return dict(tokens=tokens, w_gate=w_gate, w_up=w_up, w_down=w_down, route_ids=route_ids, route_scores=route_scores, norm_gain=norm_gain, class_head=class_head, targets=targets)


LOSS_SCALE = 8.0
NORM_EPS = 1e-06

def silu_parts(gate_act):
    sigmoid_gate = jax.nn.sigmoid(gate_act)
    return (gate_act * sigmoid_gate, sigmoid_gate * (1.0 + gate_act * (1.0 - sigmoid_gate)))

def reference(tokens, w_gate, w_up, w_down, route_ids, route_scores, norm_gain, class_head, targets):
    token_float = tokens.astype(jnp.float32).reshape(SEQS, TOK_DEV, D)
    expert_ids = route_ids.reshape(SEQS, TOK_DEV, TOP)
    route_weight = (route_scores / lax.optimization_barrier(jnp.sum(route_scores, axis=-1, keepdims=True))).reshape(SEQS, TOK_DEV, TOP)
    expert_iota = jnp.arange(EXPERTS, dtype=jnp.int32)
    matches = (expert_ids[..., None] == expert_iota).astype(jnp.int32)
    named_count = lax.optimization_barrier(jnp.sum(matches, axis=2))
    before = jnp.cumsum(named_count, axis=1) - named_count
    weight_by = lax.optimization_barrier(jnp.sum(matches.astype(jnp.float32) * route_weight[..., None], axis=2))
    slot_iota = jnp.arange(CAP, dtype=jnp.int32)

    def placement(expert):
        chosen = named_count[:, :, expert]
        slot_pos = before[:, :, expert]
        hit = (slot_pos[:, None, :] == slot_iota[None, :, None]) & (chosen[:, None, :] == 1)
        return hit.astype(jnp.float32)

    def expert_rows(placement_map):
        slot_rows = jnp.einsum('sct,std->scd', placement_map, token_float)
        return slot_rows.astype(jnp.bfloat16).reshape(SEQS * CAP, D)

    def forward_expert(running, expert):
        placement_map = placement(expert)
        slot_rows = expert_rows(placement_map)
        gate_act = jnp.dot(slot_rows, w_gate[expert], preferred_element_type=jnp.float32)
        up_act = jnp.dot(slot_rows, w_up[expert], preferred_element_type=jnp.float32)
        silu_val, silu_slope = silu_parts(gate_act)
        hidden = (silu_val * up_act).astype(jnp.bfloat16)
        expert_out = jnp.dot(hidden, w_down[expert], preferred_element_type=jnp.float32).astype(jnp.bfloat16)
        weighted_place = placement_map * weight_by[:, :, expert][:, None, :]
        expert_float = expert_out.astype(jnp.float32).reshape(SEQS, CAP, D)
        running = running + jnp.einsum('sct,scd->std', weighted_place, expert_float)
        return (running, None)
    moe_out, _ = lax.scan(forward_expert, jnp.zeros((SEQS, TOK_DEV, D), jnp.float32), expert_iota)
    residual = token_float + moe_out
    inv_rms = lax.rsqrt(lax.optimization_barrier(jnp.mean(residual * residual, axis=-1, keepdims=True)) + NORM_EPS)
    normed = residual * inv_rms * norm_gain
    pooled = lax.optimization_barrier(jnp.mean(normed, axis=1)).astype(jnp.bfloat16)
    logits = jnp.dot(pooled, class_head, preferred_element_type=jnp.float32)
    target_rows = targets.reshape(SEQS, LABELS).astype(jnp.float32)
    logit_grad = (LOSS_SCALE * (jax.nn.sigmoid(logits) - target_rows)).astype(jnp.bfloat16)
    head_grad = jnp.dot(pooled.T, logit_grad, preferred_element_type=jnp.float32)
    pooled_grad = jnp.dot(logit_grad, class_head.T, preferred_element_type=jnp.float32)
    scaled = norm_gain * pooled_grad[:, None, :] / TOK_DEV
    cube = inv_rms * inv_rms * inv_rms
    resid_grad = inv_rms * scaled - residual * cube * lax.optimization_barrier(jnp.mean(residual * scaled, axis=-1, keepdims=True))

    def backward_expert(running, expert):
        placement_map = placement(expert)
        slot_rows = expert_rows(placement_map)
        gate_act = jnp.dot(slot_rows, w_gate[expert], preferred_element_type=jnp.float32)
        up_act = jnp.dot(slot_rows, w_up[expert], preferred_element_type=jnp.float32)
        silu_val, silu_slope = silu_parts(gate_act)
        weighted_place = placement_map * weight_by[:, :, expert][:, None, :]
        slot_grad = jnp.einsum('sct,std->scd', weighted_place, resid_grad).astype(jnp.bfloat16).reshape(SEQS * CAP, D)
        down_back = jnp.dot(slot_grad, w_down[expert].T, preferred_element_type=jnp.float32)
        gate_grad = (down_back * up_act * silu_slope).astype(jnp.bfloat16)
        up_grad = (down_back * silu_val).astype(jnp.bfloat16)
        input_grad = jnp.dot(gate_grad, w_gate[expert].T, preferred_element_type=jnp.float32)
        input_grad = input_grad + jnp.dot(up_grad, w_up[expert].T, preferred_element_type=jnp.float32)
        input_grad = input_grad.astype(jnp.bfloat16).astype(jnp.float32).reshape(SEQS, CAP, D)
        running = running + jnp.einsum('sct,scd->std', placement_map, input_grad)
        return (running, None)
    expert_grads, _ = lax.scan(backward_expert, jnp.zeros((SEQS, TOK_DEV, D), jnp.float32), expert_iota)
    token_grad = (resid_grad + expert_grads).astype(jnp.bfloat16).reshape(TOKENS, D)
    return (token_grad, head_grad)
```

```python
import functools

import jax
import jax.numpy as jnp
from jax import lax
from jax.experimental import pallas as pl
from jax.experimental.pallas import tpu as pltpu
from jax.sharding import PartitionSpec as P

LOSS_SCALE = 8.0
NORM_EPS = 1e-06
LANES = 128
HALF = 64
NT = (((1,), (1,)), ((), ()))


def ring_place(expert, n, snake):
    if not snake:
        return expert
    odd = lax.rem(expert, 2)
    return (1 - odd) * (expert // 2) + odd * (n - 1 - expert // 2)


def ring_expert(place, n, snake):
    if not snake:
        return place
    back = place // (n // 2)
    return (1 - back) * 2 * place + back * (2 * n - 1 - 2 * place)


def kernel(
    n,
    groups,
    gather_weights,
    snake,
    tok_ref,
    ids_ref,
    score_ref,
    gain_ref,
    head_ref,
    target_ref,
    wg_ref,
    wu_ref,
    wd_ref,
    out_ref,
    pool_ref,
    lg_ref,
    wg,
    wu,
    wd,
    xbuf,
    gbuf,
    gate_coef,
    up_coef,
    part,
    from_right,
    from_left,
    resid,
    pool_mine,
    pool_all,
    terms,
    terms_in,
    w_local_sem,
    w_send_sem,
    w_recv_sem,
    cw_send,
    ccw_send,
    ring_recv,
    left_send,
    right_send,
    left_recv,
    right_recv,
    small_send,
    small_recv,
    group_send,
    group_recv,
):
    rows, width = tok_ref.shape
    local, _, hidden = wg.shape
    half = n // 2
    expert = lax.axis_index("expert")
    group = lax.axis_index("group")
    place = ring_place(expert, n, snake)
    right = ring_expert(lax.rem(place + 1, n), n, snake)
    left = ring_expert(lax.rem(place + n - 1, n), n, snake)

    barrier = pltpu.get_barrier_semaphore()
    for off in range(1, n):
        pl.semaphore_signal(barrier, inc=1, device_id={"expert": lax.rem(expert + off, n)})
    for off in range(1, groups):
        pl.semaphore_signal(barrier, inc=1, device_id={"group": lax.rem(group + off, groups)})

    locals_ = []
    for i, (src, dst) in enumerate(((wg_ref, wg), (wu_ref, wu), (wd_ref, wd))):
        span = src.shape[1]
        at = pl.multiple_of(group * span, 16) if gather_weights else 0
        copy = pltpu.make_async_copy(src, dst.at[:, pl.ds(at, span), :], w_local_sem.at[i])
        copy.start()
        locals_.append(copy)

    ids = ids_ref[...]
    score = score_ref[...]
    weight = score / jnp.sum(score, axis=-1, keepdims=True)
    lane = lax.rem(lax.broadcasted_iota(jnp.int32, (rows, LANES), 1), HALF)
    low = lax.broadcasted_iota(jnp.int32, (rows, LANES), 1) < HALF
    by_expert = jnp.zeros((rows, LANES), jnp.float32)
    for k in range(ids.shape[1]):
        by_expert += jnp.where(lane == ids[:, k : k + 1], weight[:, k : k + 1], 0.0)
    high_part = by_expert.astype(jnp.bfloat16).astype(jnp.float32)
    xbuf[0, :, :width] = tok_ref[...]
    xbuf[0, :, width:] = jnp.where(low, high_part, by_expert - high_part).astype(jnp.bfloat16)

    pl.semaphore_wait(barrier, n - 1 + groups - 1)

    def cw(buf, phase, k):
        return pltpu.make_async_remote_copy(
            src_ref=buf.at[k],
            dst_ref=buf.at[k + 1],
            send_sem=cw_send.at[phase, k],
            recv_sem=ring_recv.at[phase, k + 1],
            device_id={"expert": right},
        )

    def ccw(buf, phase, k):
        return pltpu.make_async_remote_copy(
            src_ref=buf.at[lax.rem(k, n)],
            dst_ref=buf.at[k - 1],
            send_sem=ccw_send.at[phase, k - 1],
            recv_sem=ring_recv.at[phase, k - 1],
            device_id={"expert": left},
        )

    cw(xbuf, 0, 0).start()
    ccw(xbuf, 0, n).start()

    w_copies = []
    if gather_weights:
        for off in range(1, groups):
            for i, (src, dst) in enumerate(((wg_ref, wg), (wu_ref, wu), (wd_ref, wd))):
                span = src.shape[1]
                at = pl.multiple_of(group * span, 16)
                copy = pltpu.make_async_remote_copy(
                    src_ref=src,
                    dst_ref=dst.at[:, pl.ds(at, span), :],
                    send_sem=w_send_sem.at[off, i],
                    recv_sem=w_recv_sem.at[off, i],
                    device_id={"group": lax.rem(group + off, groups)},
                )
                copy.start()
                w_copies.append(copy)
    for copy in locals_:
        copy.wait()
    for copy in w_copies:
        copy.wait()

    def forward_block(k):
        x = xbuf[k, :, :width]
        ext = xbuf[k, :, width:].astype(jnp.float32)
        total = jnp.zeros((rows, width), jnp.float32)
        for j in range(local):
            w = jnp.sum(jnp.where(lane == expert * local + j, ext, 0.0), axis=1, keepdims=True)
            gate = jnp.dot(x, wg[j], preferred_element_type=jnp.float32)
            up = jnp.dot(x, wu[j], preferred_element_type=jnp.float32)
            sig = 1.0 / (1.0 + jnp.exp(-gate))
            silu = gate * sig * w
            gate_coef[k, j] = up * (sig * (1.0 + gate * (1.0 - sig))) * w
            up_coef[k, j] = silu
            total += jnp.dot(
                (silu * up).astype(jnp.bfloat16), wd[j], preferred_element_type=jnp.float32
            )
        part[0, k] = total.astype(jnp.bfloat16)

    def backward_block(k):
        g = gbuf[k]
        total = jnp.zeros((rows, width), jnp.float32)
        for j in range(local):
            back = lax.dot_general(g, wd[j], NT, preferred_element_type=jnp.float32)
            gate_grad = (back * gate_coef[k, j]).astype(jnp.bfloat16)
            up_grad = (back * up_coef[k, j]).astype(jnp.bfloat16)
            total += lax.dot_general(gate_grad, wg[j], NT, preferred_element_type=jnp.float32)
            total += lax.dot_general(up_grad, wu[j], NT, preferred_element_type=jnp.float32)
        part[1, k] = total.astype(jnp.bfloat16)

    def gather_phase(buf, phase, block):
        def step(i, carry):
            s = (i + 1) // 2
            odd = lax.rem(i, 2)

            @pl.when(odd == 1)
            def _():
                cw(buf, phase, s - 1).wait_recv()

                @pl.when(s < half)
                def _():
                    cw(buf, phase, s).start()
                    ccw(buf, phase, n - s + 1).wait_recv()

                    @pl.when(s < half - 1)
                    def _():
                        ccw(buf, phase, n - s).start()

            block(odd * s + (1 - odd) * lax.rem(n - s, n))
            return carry

        lax.fori_loop(0, n, step, 0)

        def drain_cw(k, carry):
            cw(buf, phase, k).wait_send()
            return carry

        def drain_ccw(k, carry):
            ccw(buf, phase, n - k).wait_send()
            return carry

        lax.fori_loop(0, half, drain_cw, 0)
        lax.fori_loop(0, half - 1, drain_ccw, 0)

    def to_left(phase, k):
        return pltpu.make_async_remote_copy(
            src_ref=part.at[phase, k],
            dst_ref=from_right.at[phase, k - 1],
            send_sem=left_send.at[phase, k],
            recv_sem=left_recv.at[phase, k - 1],
            device_id={"expert": left},
        )

    def to_right(phase, d):
        return pltpu.make_async_remote_copy(
            src_ref=part.at[phase, n - d],
            dst_ref=from_left.at[phase, d - 1],
            send_sem=right_send.at[phase, d],
            recv_sem=right_recv.at[phase, d - 1],
            device_id={"expert": right},
        )

    def reduce_phase(phase):
        to_left(phase, half).start()
        to_right(phase, half - 1).start()

        def step(s, carry):
            k = half - s
            to_left(phase, k + 1).wait_recv()
            part[phase, k] = (
                part[phase, k].astype(jnp.float32) + from_right[phase, k].astype(jnp.float32)
            ).astype(jnp.bfloat16)
            to_left(phase, k).start()

            @pl.when(s < half - 1)
            def _():
                d = half - 1 - s
                to_right(phase, d + 1).wait_recv()
                part[phase, n - d] = (
                    part[phase, n - d].astype(jnp.float32)
                    + from_left[phase, d].astype(jnp.float32)
                ).astype(jnp.bfloat16)
                to_right(phase, d).start()

            return carry

        lax.fori_loop(1, half, step, 0)
        to_right(phase, 1).wait_recv()
        to_left(phase, 1).wait_recv()

        def drain_left(k, carry):
            to_left(phase, k).wait_send()
            return carry

        def drain_right(d, carry):
            to_right(phase, d).wait_send()
            return carry

        lax.fori_loop(1, half + 1, drain_left, 0)
        lax.fori_loop(1, half, drain_right, 0)
        return (
            part[phase, 0].astype(jnp.float32)
            + from_right[phase, 0].astype(jnp.float32)
            + from_left[phase, 0].astype(jnp.float32)
        )

    gather_phase(xbuf, 0, forward_block)
    residual = xbuf[0, :, :width].astype(jnp.float32) + reduce_phase(0)
    gain = gain_ref[...]
    inv_rms = lax.rsqrt(jnp.mean(residual * residual, axis=-1, keepdims=True) + NORM_EPS)
    resid[...] = residual
    pooled = jnp.sum(residual * inv_rms * gain, axis=0, keepdims=True) / rows
    pooled = pooled.astype(jnp.bfloat16).astype(jnp.float32)
    pool_mine[...] = pooled
    pool_all[pl.ds(expert, 1)] = pooled[None]

    def small(i, src, dst, off):
        return pltpu.make_async_remote_copy(
            src_ref=src,
            dst_ref=dst,
            send_sem=small_send.at[i, off],
            recv_sem=small_recv.at[i, off],
            device_id={"expert": lax.rem(expert + off, n)},
        )

    copies = [small(0, pool_mine, pool_all.at[expert], off) for off in range(1, n)]
    for copy in copies:
        copy.start()
    for copy in copies:
        copy.wait()
    pooled_rows = jnp.concatenate([pool_all[i] for i in range(n)], axis=0).astype(jnp.bfloat16)
    logits = jnp.dot(pooled_rows, head_ref[...], preferred_element_type=jnp.float32)
    sig = 1.0 / (1.0 + jnp.exp(-logits))
    logit_grad = (LOSS_SCALE * (sig - target_ref[...].astype(jnp.float32))).astype(jnp.bfloat16)
    pooled_terms = lax.dot_general(logit_grad, head_ref[...], NT, preferred_element_type=jnp.float32)
    for i in range(n):
        terms[i] = pooled_terms[i : i + 1, :]
    copies = [
        small(1, terms.at[lax.rem(expert + off, n)], terms_in.at[off], off) for off in range(1, n)
    ]
    for copy in copies:
        copy.start()
    pool_ref[pl.ds(group, 1)] = pooled_rows.astype(jnp.float32)[None]
    lg_ref[pl.ds(group, 1)] = logit_grad.astype(jnp.float32)[None]
    group_copies = []
    for off in range(1, groups):
        for i, ref in enumerate((pool_ref, lg_ref)):
            copy = pltpu.make_async_remote_copy(
                src_ref=ref.at[group],
                dst_ref=ref.at[group],
                send_sem=group_send.at[off, i],
                recv_sem=group_recv.at[off, i],
                device_id={"group": lax.rem(group + off, groups)},
            )
            copy.start()
            group_copies.append(copy)
    for copy in copies:
        copy.wait()
    pooled_grad = terms[expert]
    for off in range(1, n):
        pooled_grad = pooled_grad + terms_in[off]
    residual = resid[...]
    inv_rms = lax.rsqrt(jnp.mean(residual * residual, axis=-1, keepdims=True) + NORM_EPS)
    scaled = gain * pooled_grad / rows
    cube = inv_rms * inv_rms * inv_rms
    resid_grad = inv_rms * scaled - residual * (
        cube * jnp.mean(residual * scaled, axis=-1, keepdims=True)
    )
    gbuf[0] = resid_grad.astype(jnp.bfloat16)
    cw(gbuf, 1, 0).start()
    ccw(gbuf, 1, n).start()
    resid[...] = resid_grad
    gather_phase(gbuf, 1, backward_block)
    out_ref[...] = (resid[...] + reduce_phase(1)).astype(jnp.bfloat16)
    for copy in group_copies:
        copy.wait()


def body(tokens, w_gate, w_up, w_down, route_ids, route_scores, norm_gain, class_head, targets):
    rows, width = tokens.shape
    n = lax.axis_size("expert")
    groups = lax.axis_size("group")
    local, _, hidden = w_gate.shape
    labels = class_head.shape[1]
    half = n // 2
    gather_weights = w_gate.shape[1] % 16 == 0 and w_down.shape[1] % 16 == 0
    if not gather_weights:
        w_gate = lax.all_gather(w_gate, "group", axis=1, tiled=True)
        w_up = lax.all_gather(w_up, "group", axis=1, tiled=True)
        w_down = lax.all_gather(w_down, "group", axis=1, tiled=True)
    vmem = pl.BlockSpec(memory_space=pltpu.VMEM)
    hbm = pl.BlockSpec(memory_space=pl.ANY)
    dma = pltpu.SemaphoreType.DMA
    bf16, f32 = jnp.bfloat16, jnp.float32
    token_grad, pool, lg = pl.pallas_call(
        functools.partial(kernel, n, groups, gather_weights, n == 8),
        out_shape=(
            jax.ShapeDtypeStruct((rows, width), bf16),
            jax.ShapeDtypeStruct((groups, n, width), f32),
            jax.ShapeDtypeStruct((groups, n, labels), f32),
        ),
        in_specs=[vmem] * 6 + [hbm] * 3,
        out_specs=(vmem, vmem, vmem),
        scratch_shapes=[
            pltpu.VMEM((local, width, hidden), bf16),
            pltpu.VMEM((local, width, hidden), bf16),
            pltpu.VMEM((local, hidden, width), bf16),
            pltpu.VMEM((n, rows, width + LANES), bf16),
            pltpu.VMEM((n, rows, width), bf16),
            pltpu.VMEM((n, local, rows, hidden), f32),
            pltpu.VMEM((n, local, rows, hidden), f32),
            pltpu.VMEM((2, n, rows, width), bf16),
            pltpu.VMEM((2, half, rows, width), bf16),
            pltpu.VMEM((2, half, rows, width), bf16),
            pltpu.VMEM((rows, width), f32),
            pltpu.VMEM((1, width), f32),
            pltpu.VMEM((n, 1, width), f32),
            pltpu.VMEM((n, 1, width), f32),
            pltpu.VMEM((n, 1, width), f32),
            dma((3,)),
            dma((groups, 3)),
            dma((groups, 3)),
            dma((2, n)),
            dma((2, n)),
            dma((2, n)),
            dma((2, n)),
            dma((2, n)),
            dma((2, n)),
            dma((2, n)),
            dma((2, n)),
            dma((2, n)),
            dma((groups, 2)),
            dma((groups, 2)),
        ],
        compiler_params=pltpu.CompilerParams(
            collective_id=0, has_side_effects=True, vmem_limit_bytes=60 * 1024 * 1024
        ),
    )(
        tokens,
        route_ids,
        route_scores,
        norm_gain.reshape(1, width),
        class_head,
        targets.reshape(n, labels),
        w_gate,
        w_up,
        w_down,
    )
    head_grad = lax.dot_general(
        pool.reshape(-1, width).astype(bf16),
        lg.reshape(-1, labels).astype(bf16),
        (((0,), (0,)), ((), ())),
        preferred_element_type=f32,
    )
    return token_grad, head_grad


def solution(mesh):
    in_specs = (
        P(("rep", "expert", "group"), None),
        P("expert", "group", None),
        P("expert", "group", None),
        P("expert", "group", None),
        P(("rep", "expert", "group"), None),
        P(("rep", "expert", "group"), None),
        P(),
        P(None, "expert"),
        P("rep", "group", "expert"),
    )
    out_specs = (P(("rep", "expert", "group"), None), P("rep", "expert"))
    return jax.shard_map(body, mesh=mesh, in_specs=in_specs, out_specs=out_specs, check_vma=False)
```

```python
import functools

import jax
import jax.numpy as jnp
from jax import lax
from jax.experimental import pallas as pl
from jax.experimental.pallas import tpu as pltpu
from jax.sharding import PartitionSpec as P

LOSS_SCALE = 8.0
NORM_EPS = 1e-06
LANES = 128
HALF = 64
NT = (((1,), (1,)), ((), ()))


def ring_place(expert, n, snake):
    if not snake:
        return expert
    odd = lax.rem(expert, 2)
    return (1 - odd) * (expert // 2) + odd * (n - 1 - expert // 2)


def ring_expert(place, n, snake):
    if not snake:
        return place
    back = place // (n // 2)
    return (1 - back) * 2 * place + back * (2 * n - 1 - 2 * place)


def kernel(
    n,
    groups,
    gather_weights,
    snake,
    tok_ref,
    ids_ref,
    score_ref,
    gain_ref,
    head_ref,
    target_ref,
    wg_ref,
    wu_ref,
    wd_ref,
    out_ref,
    pool_ref,
    lg_ref,
    wg,
    wu,
    wd,
    xbuf,
    gbuf,
    gate_coef,
    up_coef,
    part,
    from_right,
    from_left,
    resid,
    pool_mine,
    pool_all,
    terms,
    terms_in,
    w_local_sem,
    w_send_sem,
    w_recv_sem,
    cw_send,
    ccw_send,
    ring_recv,
    left_send,
    right_send,
    left_recv,
    right_recv,
    small_send,
    small_recv,
    group_send,
    group_recv,
):
    rows, width = tok_ref.shape
    local, _, hidden = wg.shape
    half = n // 2
    expert = lax.axis_index("expert")
    group = lax.axis_index("group")
    place = ring_place(expert, n, snake)
    right = ring_expert(lax.rem(place + 1, n), n, snake)
    left = ring_expert(lax.rem(place + n - 1, n), n, snake)

    barrier = pltpu.get_barrier_semaphore()
    for off in range(1, n):
        pl.semaphore_signal(barrier, inc=1, device_id={"expert": lax.rem(expert + off, n)})
    for off in range(1, groups):
        pl.semaphore_signal(barrier, inc=1, device_id={"group": lax.rem(group + off, groups)})

    locals_ = []
    for i, (src, dst) in enumerate(((wg_ref, wg), (wu_ref, wu), (wd_ref, wd))):
        span = src.shape[1]
        at = pl.multiple_of(group * span, 16) if gather_weights else 0
        copy = pltpu.make_async_copy(src, dst.at[:, pl.ds(at, span), :], w_local_sem.at[i])
        copy.start()
        locals_.append(copy)

    ids = ids_ref[...]
    score = score_ref[...]
    weight = score / jnp.sum(score, axis=-1, keepdims=True)
    lane = lax.rem(lax.broadcasted_iota(jnp.int32, (rows, LANES), 1), HALF)
    low = lax.broadcasted_iota(jnp.int32, (rows, LANES), 1) < HALF
    by_expert = jnp.zeros((rows, LANES), jnp.float32)
    for k in range(ids.shape[1]):
        by_expert += jnp.where(lane == ids[:, k : k + 1], weight[:, k : k + 1], 0.0)
    high_part = by_expert.astype(jnp.bfloat16).astype(jnp.float32)
    xbuf[0, :, :width] = tok_ref[...]
    xbuf[0, :, width:] = jnp.where(low, high_part, by_expert - high_part).astype(jnp.bfloat16)

    pl.semaphore_wait(barrier, n - 1 + groups - 1)

    piece = rows // 2

    def chunk(buf, at, c):
        return buf.at[(*at, pl.ds(c * piece, piece))]

    def cw(buf, phase, k, c):
        return pltpu.make_async_remote_copy(
            src_ref=chunk(buf, (k,), c),
            dst_ref=chunk(buf, (k + 1,), c),
            send_sem=cw_send.at[phase, c, k],
            recv_sem=ring_recv.at[phase, c, k + 1],
            device_id={"expert": right},
        )

    def ccw(buf, phase, k, c):
        return pltpu.make_async_remote_copy(
            src_ref=chunk(buf, (lax.rem(k, n),), c),
            dst_ref=chunk(buf, (k - 1,), c),
            send_sem=ccw_send.at[phase, c, k - 1],
            recv_sem=ring_recv.at[phase, c, k - 1],
            device_id={"expert": left},
        )

    for c in range(2):
        cw(xbuf, 0, 0, c).start()
        ccw(xbuf, 0, n, c).start()

    w_copies = []
    if gather_weights:
        for off in range(1, groups):
            for i, (src, dst) in enumerate(((wg_ref, wg), (wu_ref, wu), (wd_ref, wd))):
                span = src.shape[1]
                at = pl.multiple_of(group * span, 16)
                copy = pltpu.make_async_remote_copy(
                    src_ref=src,
                    dst_ref=dst.at[:, pl.ds(at, span), :],
                    send_sem=w_send_sem.at[off, i],
                    recv_sem=w_recv_sem.at[off, i],
                    device_id={"group": lax.rem(group + off, groups)},
                )
                copy.start()
                w_copies.append(copy)

    def weights_ready():
        for copy in locals_:
            copy.wait()
        for copy in w_copies:
            copy.wait()

    def forward_block(k):
        x = xbuf[k, :, :width]
        ext = xbuf[k, :, width:].astype(jnp.float32)
        total = jnp.zeros((rows, width), jnp.float32)
        for j in range(local):
            w = jnp.sum(jnp.where(lane == expert * local + j, ext, 0.0), axis=1, keepdims=True)
            gate = jnp.dot(x, wg[j], preferred_element_type=jnp.float32)
            up = jnp.dot(x, wu[j], preferred_element_type=jnp.float32)
            sig = 1.0 / (1.0 + jnp.exp(-gate))
            silu = gate * sig * w
            gate_coef[k, j] = up * (sig * (1.0 + gate * (1.0 - sig))) * w
            up_coef[k, j] = silu
            total += jnp.dot(
                (silu * up).astype(jnp.bfloat16), wd[j], preferred_element_type=jnp.float32
            )
        part[0, k] = total.astype(jnp.bfloat16)

    def backward_block(k):
        g = gbuf[k]
        total = jnp.zeros((rows, width), jnp.float32)
        for j in range(local):
            back = lax.dot_general(g, wd[j], NT, preferred_element_type=jnp.float32)
            gate_grad = (back * gate_coef[k, j]).astype(jnp.bfloat16)
            up_grad = (back * up_coef[k, j]).astype(jnp.bfloat16)
            total += lax.dot_general(gate_grad, wg[j], NT, preferred_element_type=jnp.float32)
            total += lax.dot_general(up_grad, wu[j], NT, preferred_element_type=jnp.float32)
        part[1, k] = total.astype(jnp.bfloat16)

    def gather_phase(buf, phase, block, ready):
        def arrive(s):
            for c in range(2):
                cw(buf, phase, s - 1, c).wait_recv()

                @pl.when((s < half - 1) | (c == 0))
                def _():
                    cw(buf, phase, s, c).start()

                ccw(buf, phase, n - s + 1, c).wait_recv()

                @pl.when((s < half - 1) | (c == 1))
                def _():
                    ccw(buf, phase, n - s, c).start()

        arrive(jnp.int32(1))
        ready()

        def step(i, carry):
            s = (i + 1) // 2
            odd = lax.rem(i, 2)

            @pl.when((odd == 1) & (s > 1) & (s < half))
            def _():
                arrive(s)

            @pl.when((odd == 1) & (s == half))
            def _():
                cw(buf, phase, half - 1, 0).wait_recv()
                ccw(buf, phase, half + 1, 1).wait_recv()

            block(odd * s + (1 - odd) * lax.rem(n - s, n))
            return carry

        lax.fori_loop(0, n, step, 0)
        for c in range(2):

            def drain_cw(k, carry):
                cw(buf, phase, k, c).wait_send()
                return carry

            def drain_ccw(k, carry):
                ccw(buf, phase, n - k, c).wait_send()
                return carry

            lax.fori_loop(0, half - c, drain_cw, 0)
            lax.fori_loop(0, half - 1 + c, drain_ccw, 0)

    def to_left(phase, k, c):
        return pltpu.make_async_remote_copy(
            src_ref=chunk(part, (phase, k), c),
            dst_ref=chunk(from_right, (phase, k - 1), c),
            send_sem=left_send.at[phase, c, k],
            recv_sem=left_recv.at[phase, c, k - 1],
            device_id={"expert": left},
        )

    def to_right(phase, d, c):
        return pltpu.make_async_remote_copy(
            src_ref=chunk(part, (phase, n - d), c),
            dst_ref=chunk(from_left, (phase, d - 1), c),
            send_sem=right_send.at[phase, c, d],
            recv_sem=right_recv.at[phase, c, d - 1],
            device_id={"expert": right},
        )

    def add_piece(phase, slot, incoming, at, c):
        span = pl.ds(c * piece, piece)
        part[phase, slot, span] = (
            part[phase, slot, span].astype(jnp.float32)
            + incoming[phase, at, span].astype(jnp.float32)
        ).astype(jnp.bfloat16)

    def reduce_phase(phase):
        to_left(phase, half, 0).start()
        to_right(phase, half, 1).start()
        to_right(phase, half - 1, 0).start()
        to_left(phase, half - 1, 1).start()

        def pass_left(k, c):
            to_left(phase, k + 1, c).wait_recv()
            add_piece(phase, k, from_right, k, c)
            to_left(phase, k, c).start()

        def pass_right(d, c):
            to_right(phase, d + 1, c).wait_recv()
            add_piece(phase, n - d, from_left, d, c)
            to_right(phase, d, c).start()

        def step(s, carry):
            pass_left(half - s, 0)
            pass_right(half - s, 1)

            @pl.when(s < half - 1)
            def _():
                pass_right(half - 1 - s, 0)
                pass_left(half - 1 - s, 1)

            return carry

        lax.fori_loop(1, half, step, 0)
        for c in range(2):
            to_right(phase, 1, c).wait_recv()
            to_left(phase, 1, c).wait_recv()

            def drain_left(k, carry):
                to_left(phase, k, c).wait_send()
                return carry

            def drain_right(d, carry):
                to_right(phase, d, c).wait_send()
                return carry

            lax.fori_loop(1, half + 1 - c, drain_left, 0)
            lax.fori_loop(1, half + c, drain_right, 0)
        return (
            part[phase, 0].astype(jnp.float32)
            + from_right[phase, 0].astype(jnp.float32)
            + from_left[phase, 0].astype(jnp.float32)
        )

    gather_phase(xbuf, 0, forward_block, weights_ready)
    residual = xbuf[0, :, :width].astype(jnp.float32) + reduce_phase(0)
    gain = gain_ref[...]
    inv_rms = lax.rsqrt(jnp.mean(residual * residual, axis=-1, keepdims=True) + NORM_EPS)
    resid[...] = residual
    pooled = jnp.sum(residual * inv_rms * gain, axis=0, keepdims=True) / rows
    pooled = pooled.astype(jnp.bfloat16).astype(jnp.float32)
    pool_mine[...] = pooled
    pool_all[pl.ds(expert, 1)] = pooled[None]

    def small(i, src, dst, off):
        return pltpu.make_async_remote_copy(
            src_ref=src,
            dst_ref=dst,
            send_sem=small_send.at[i, off],
            recv_sem=small_recv.at[i, off],
            device_id={"expert": lax.rem(expert + off, n)},
        )

    copies = [small(0, pool_mine, pool_all.at[expert], off) for off in range(1, n)]
    for copy in copies:
        copy.start()
    for copy in copies:
        copy.wait()
    pooled_rows = jnp.concatenate([pool_all[i] for i in range(n)], axis=0).astype(jnp.bfloat16)
    logits = jnp.dot(pooled_rows, head_ref[...], preferred_element_type=jnp.float32)
    sig = 1.0 / (1.0 + jnp.exp(-logits))
    logit_grad = (LOSS_SCALE * (sig - target_ref[...].astype(jnp.float32))).astype(jnp.bfloat16)
    pooled_terms = lax.dot_general(logit_grad, head_ref[...], NT, preferred_element_type=jnp.float32)
    for i in range(n):
        terms[i] = pooled_terms[i : i + 1, :]
    copies = [
        small(1, terms.at[lax.rem(expert + off, n)], terms_in.at[off], off) for off in range(1, n)
    ]
    for copy in copies:
        copy.start()
    pool_ref[pl.ds(group, 1)] = pooled_rows.astype(jnp.float32)[None]
    lg_ref[pl.ds(group, 1)] = logit_grad.astype(jnp.float32)[None]
    group_copies = []
    for off in range(1, groups):
        for i, ref in enumerate((pool_ref, lg_ref)):
            copy = pltpu.make_async_remote_copy(
                src_ref=ref.at[group],
                dst_ref=ref.at[group],
                send_sem=group_send.at[off, i],
                recv_sem=group_recv.at[off, i],
                device_id={"group": lax.rem(group + off, groups)},
            )
            copy.start()
            group_copies.append(copy)
    for copy in copies:
        copy.wait()
    pooled_grad = terms[expert]
    for off in range(1, n):
        pooled_grad = pooled_grad + terms_in[off]
    residual = resid[...]
    inv_rms = lax.rsqrt(jnp.mean(residual * residual, axis=-1, keepdims=True) + NORM_EPS)
    scaled = gain * pooled_grad / rows
    cube = inv_rms * inv_rms * inv_rms
    resid_grad = inv_rms * scaled - residual * (
        cube * jnp.mean(residual * scaled, axis=-1, keepdims=True)
    )
    gbuf[0] = resid_grad.astype(jnp.bfloat16)
    for c in range(2):
        cw(gbuf, 1, 0, c).start()
        ccw(gbuf, 1, n, c).start()
    resid[...] = resid_grad
    gather_phase(gbuf, 1, backward_block, lambda: None)
    out_ref[...] = (resid[...] + reduce_phase(1)).astype(jnp.bfloat16)
    for copy in group_copies:
        copy.wait()


def body(tokens, w_gate, w_up, w_down, route_ids, route_scores, norm_gain, class_head, targets):
    rows, width = tokens.shape
    n = lax.axis_size("expert")
    groups = lax.axis_size("group")
    local, _, hidden = w_gate.shape
    labels = class_head.shape[1]
    half = n // 2
    gather_weights = w_gate.shape[1] % 16 == 0 and w_down.shape[1] % 16 == 0
    if not gather_weights:
        w_gate = lax.all_gather(w_gate, "group", axis=1, tiled=True)
        w_up = lax.all_gather(w_up, "group", axis=1, tiled=True)
        w_down = lax.all_gather(w_down, "group", axis=1, tiled=True)
    vmem = pl.BlockSpec(memory_space=pltpu.VMEM)
    hbm = pl.BlockSpec(memory_space=pl.ANY)
    dma = pltpu.SemaphoreType.DMA
    bf16, f32 = jnp.bfloat16, jnp.float32
    token_grad, pool, lg = pl.pallas_call(
        functools.partial(kernel, n, groups, gather_weights, n == 8),
        out_shape=(
            jax.ShapeDtypeStruct((rows, width), bf16),
            jax.ShapeDtypeStruct((groups, n, width), f32),
            jax.ShapeDtypeStruct((groups, n, labels), f32),
        ),
        in_specs=[vmem] * 6 + [hbm] * 3,
        out_specs=(vmem, vmem, vmem),
        scratch_shapes=[
            pltpu.VMEM((local, width, hidden), bf16),
            pltpu.VMEM((local, width, hidden), bf16),
            pltpu.VMEM((local, hidden, width), bf16),
            pltpu.VMEM((n, rows, width + LANES), bf16),
            pltpu.VMEM((n, rows, width), bf16),
            pltpu.VMEM((n, local, rows, hidden), f32),
            pltpu.VMEM((n, local, rows, hidden), f32),
            pltpu.VMEM((2, n, rows, width), bf16),
            pltpu.VMEM((2, half, rows, width), bf16),
            pltpu.VMEM((2, half, rows, width), bf16),
            pltpu.VMEM((rows, width), f32),
            pltpu.VMEM((1, width), f32),
            pltpu.VMEM((n, 1, width), f32),
            pltpu.VMEM((n, 1, width), f32),
            pltpu.VMEM((n, 1, width), f32),
            dma((3,)),
            dma((groups, 3)),
            dma((groups, 3)),
            dma((2, 2, n)),
            dma((2, 2, n)),
            dma((2, 2, n)),
            dma((2, 2, n)),
            dma((2, 2, n)),
            dma((2, 2, n)),
            dma((2, 2, n)),
            dma((2, n)),
            dma((2, n)),
            dma((groups, 2)),
            dma((groups, 2)),
        ],
        compiler_params=pltpu.CompilerParams(
            collective_id=0, has_side_effects=True, vmem_limit_bytes=60 * 1024 * 1024
        ),
    )(
        tokens,
        route_ids,
        route_scores,
        norm_gain.reshape(1, width),
        class_head,
        targets.reshape(n, labels),
        w_gate,
        w_up,
        w_down,
    )
    head_grad = lax.dot_general(
        pool.reshape(-1, width).astype(bf16),
        lg.reshape(-1, labels).astype(bf16),
        (((0,), (0,)), ((), ())),
        preferred_element_type=f32,
    )
    return token_grad, head_grad


def solution(mesh):
    in_specs = (
        P(("rep", "expert", "group"), None),
        P("expert", "group", None),
        P("expert", "group", None),
        P("expert", "group", None),
        P(("rep", "expert", "group"), None),
        P(("rep", "expert", "group"), None),
        P(),
        P(None, "expert"),
        P("rep", "group", "expert"),
    )
    out_specs = (P(("rep", "expert", "group"), None), P("rep", "expert"))
    return jax.shard_map(body, mesh=mesh, in_specs=in_specs, out_specs=out_specs, check_vma=False)
```

```python
import functools

import jax
import jax.numpy as jnp
from jax import lax
from jax.experimental import pallas as pl
from jax.experimental.pallas import tpu as pltpu
from jax.sharding import PartitionSpec as P

LOSS_SCALE = 8.0
NORM_EPS = 1e-06
LANES = 128
HALF = 64
NT = (((1,), (1,)), ((), ()))


def ring_place(expert, n, snake):
    if not snake:
        return expert
    odd = lax.rem(expert, 2)
    return (1 - odd) * (expert // 2) + odd * (n - 1 - expert // 2)


def ring_expert(place, n, snake):
    if not snake:
        return place
    back = place // (n // 2)
    return (1 - back) * 2 * place + back * (2 * n - 1 - 2 * place)


def kernel(
    n,
    groups,
    gather_weights,
    snake,
    tok_ref,
    ids_ref,
    score_ref,
    gain_ref,
    head_ref,
    target_ref,
    wg_ref,
    wu_ref,
    wd_ref,
    out_ref,
    pool_ref,
    lg_ref,
    wg,
    wu,
    wd,
    xbuf,
    gbuf,
    gate_coef,
    up_coef,
    part,
    from_right,
    from_left,
    resid,
    pool_mine,
    pool_all,
    terms,
    terms_in,
    w_local_sem,
    w_send_sem,
    w_recv_sem,
    cw_send,
    ccw_send,
    ring_recv,
    left_send,
    right_send,
    left_recv,
    right_recv,
    small_send,
    small_recv,
    group_send,
    group_recv,
):
    rows, width = tok_ref.shape
    local, _, hidden = wg.shape
    half = n // 2
    expert = lax.axis_index("expert")
    group = lax.axis_index("group")
    place = ring_place(expert, n, snake)
    right = ring_expert(lax.rem(place + 1, n), n, snake)
    left = ring_expert(lax.rem(place + n - 1, n), n, snake)

    barrier = pltpu.get_barrier_semaphore()
    for off in range(1, n):
        pl.semaphore_signal(barrier, inc=1, device_id={"expert": lax.rem(expert + off, n)})
    for off in range(1, groups):
        pl.semaphore_signal(barrier, inc=1, device_id={"group": lax.rem(group + off, groups)})

    locals_ = []
    for i, (src, dst) in enumerate(((wg_ref, wg), (wu_ref, wu), (wd_ref, wd))):
        span = src.shape[1]
        at = pl.multiple_of(group * span, 16) if gather_weights else 0
        copy = pltpu.make_async_copy(src, dst.at[:, pl.ds(at, span), :], w_local_sem.at[i])
        copy.start()
        locals_.append(copy)

    ids = ids_ref[...]
    score = score_ref[...]
    weight = score / jnp.sum(score, axis=-1, keepdims=True)
    lane = lax.rem(lax.broadcasted_iota(jnp.int32, (rows, LANES), 1), HALF)
    low = lax.broadcasted_iota(jnp.int32, (rows, LANES), 1) < HALF
    by_expert = jnp.zeros((rows, LANES), jnp.float32)
    for k in range(ids.shape[1]):
        by_expert += jnp.where(lane == ids[:, k : k + 1], weight[:, k : k + 1], 0.0)
    high_part = by_expert.astype(jnp.bfloat16).astype(jnp.float32)
    xbuf[0, :, :width] = tok_ref[...]
    xbuf[0, :, width:] = jnp.where(low, high_part, by_expert - high_part).astype(jnp.bfloat16)

    pl.semaphore_wait(barrier, n - 1 + groups - 1)

    pieces = 4
    piece = rows // pieces
    turn = pieces // 2

    def chunk(buf, at, c):
        return buf.at[(*at, pl.ds(c * piece, piece))]

    def cw(buf, phase, k, c):
        return pltpu.make_async_remote_copy(
            src_ref=chunk(buf, (k,), c),
            dst_ref=chunk(buf, (k + 1,), c),
            send_sem=cw_send.at[phase, c, k],
            recv_sem=ring_recv.at[phase, c, k + 1],
            device_id={"expert": right},
        )

    def ccw(buf, phase, k, c):
        return pltpu.make_async_remote_copy(
            src_ref=chunk(buf, (lax.rem(k, n),), c),
            dst_ref=chunk(buf, (k - 1,), c),
            send_sem=ccw_send.at[phase, c, k - 1],
            recv_sem=ring_recv.at[phase, c, k - 1],
            device_id={"expert": left},
        )

    for c in range(pieces):
        cw(xbuf, 0, 0, c).start()
        ccw(xbuf, 0, n, c).start()

    w_copies = []
    if gather_weights:
        for off in range(1, groups):
            for i, (src, dst) in enumerate(((wg_ref, wg), (wu_ref, wu), (wd_ref, wd))):
                span = src.shape[1]
                at = pl.multiple_of(group * span, 16)
                copy = pltpu.make_async_remote_copy(
                    src_ref=src,
                    dst_ref=dst.at[:, pl.ds(at, span), :],
                    send_sem=w_send_sem.at[off, i],
                    recv_sem=w_recv_sem.at[off, i],
                    device_id={"group": lax.rem(group + off, groups)},
                )
                copy.start()
                w_copies.append(copy)

    def weights_ready():
        for copy in locals_:
            copy.wait()
        for copy in w_copies:
            copy.wait()

    def forward_block(k):
        x = xbuf[k, :, :width]
        ext = xbuf[k, :, width:].astype(jnp.float32)
        total = jnp.zeros((rows, width), jnp.float32)
        for j in range(local):
            w = jnp.sum(jnp.where(lane == expert * local + j, ext, 0.0), axis=1, keepdims=True)
            gate = jnp.dot(x, wg[j], preferred_element_type=jnp.float32)
            up = jnp.dot(x, wu[j], preferred_element_type=jnp.float32)
            sig = 1.0 / (1.0 + jnp.exp(-gate))
            silu = gate * sig * w
            gate_coef[k, j] = up * (sig * (1.0 + gate * (1.0 - sig))) * w
            up_coef[k, j] = silu
            total += jnp.dot(
                (silu * up).astype(jnp.bfloat16), wd[j], preferred_element_type=jnp.float32
            )
        part[0, k] = total.astype(jnp.bfloat16)

    def backward_block(k):
        g = gbuf[k]
        total = jnp.zeros((rows, width), jnp.float32)
        for j in range(local):
            back = lax.dot_general(g, wd[j], NT, preferred_element_type=jnp.float32)
            gate_grad = (back * gate_coef[k, j]).astype(jnp.bfloat16)
            up_grad = (back * up_coef[k, j]).astype(jnp.bfloat16)
            total += lax.dot_general(gate_grad, wg[j], NT, preferred_element_type=jnp.float32)
            total += lax.dot_general(up_grad, wu[j], NT, preferred_element_type=jnp.float32)
        part[1, k] = total.astype(jnp.bfloat16)

    def gather_phase(buf, phase, block, ready):
        def arrive(s):
            for c in range(pieces):
                cw(buf, phase, s - 1, c).wait_recv()

                @pl.when((s < half - 1) | (c < turn))
                def _():
                    cw(buf, phase, s, c).start()

                ccw(buf, phase, n - s + 1, c).wait_recv()

                @pl.when((s < half - 1) | (c >= turn))
                def _():
                    ccw(buf, phase, n - s, c).start()

        arrive(jnp.int32(1))
        ready()

        def step(i, carry):
            s = (i + 1) // 2
            odd = lax.rem(i, 2)

            @pl.when((odd == 1) & (s > 1) & (s < half))
            def _():
                arrive(s)

            @pl.when((odd == 1) & (s == half))
            def _():
                for c in range(turn):
                    cw(buf, phase, half - 1, c).wait_recv()
                    ccw(buf, phase, half + 1, c + turn).wait_recv()

            block(odd * s + (1 - odd) * lax.rem(n - s, n))
            return carry

        lax.fori_loop(0, n, step, 0)
        for c in range(pieces):

            def drain_cw(k, carry):
                cw(buf, phase, k, c).wait_send()
                return carry

            def drain_ccw(k, carry):
                ccw(buf, phase, n - k, c).wait_send()
                return carry

            lax.fori_loop(0, half - c // turn, drain_cw, 0)
            lax.fori_loop(0, half - 1 + c // turn, drain_ccw, 0)

    def to_left(phase, k, c):
        return pltpu.make_async_remote_copy(
            src_ref=chunk(part, (phase, k), c),
            dst_ref=chunk(from_right, (phase, k - 1), c),
            send_sem=left_send.at[phase, c, k],
            recv_sem=left_recv.at[phase, c, k - 1],
            device_id={"expert": left},
        )

    def to_right(phase, d, c):
        return pltpu.make_async_remote_copy(
            src_ref=chunk(part, (phase, n - d), c),
            dst_ref=chunk(from_left, (phase, d - 1), c),
            send_sem=right_send.at[phase, c, d],
            recv_sem=right_recv.at[phase, c, d - 1],
            device_id={"expert": right},
        )

    def add_piece(phase, slot, incoming, at, c):
        span = pl.ds(c * piece, piece)
        part[phase, slot, span] = (
            part[phase, slot, span].astype(jnp.float32)
            + incoming[phase, at, span].astype(jnp.float32)
        ).astype(jnp.bfloat16)

    def reduce_phase(phase):
        for c in range(turn):
            to_left(phase, half, c).start()
            to_right(phase, half, c + turn).start()
        for c in range(turn):
            to_right(phase, half - 1, c).start()
            to_left(phase, half - 1, c + turn).start()

        def pass_left(k, c):
            to_left(phase, k + 1, c).wait_recv()
            add_piece(phase, k, from_right, k, c)
            to_left(phase, k, c).start()

        def pass_right(d, c):
            to_right(phase, d + 1, c).wait_recv()
            add_piece(phase, n - d, from_left, d, c)
            to_right(phase, d, c).start()

        def step(s, carry):
            for c in range(turn):
                pass_left(half - s, c)
                pass_right(half - s, c + turn)

            @pl.when(s < half - 1)
            def _():
                for c in range(turn):
                    pass_right(half - 1 - s, c)
                    pass_left(half - 1 - s, c + turn)

            return carry

        lax.fori_loop(1, half, step, 0)
        for c in range(pieces):
            to_right(phase, 1, c).wait_recv()
            to_left(phase, 1, c).wait_recv()

            def drain_left(k, carry):
                to_left(phase, k, c).wait_send()
                return carry

            def drain_right(d, carry):
                to_right(phase, d, c).wait_send()
                return carry

            lax.fori_loop(1, half + 1 - c // turn, drain_left, 0)
            lax.fori_loop(1, half + c // turn, drain_right, 0)
        return (
            part[phase, 0].astype(jnp.float32)
            + from_right[phase, 0].astype(jnp.float32)
            + from_left[phase, 0].astype(jnp.float32)
        )

    gather_phase(xbuf, 0, forward_block, weights_ready)
    residual = xbuf[0, :, :width].astype(jnp.float32) + reduce_phase(0)
    gain = gain_ref[...]
    inv_rms = lax.rsqrt(jnp.mean(residual * residual, axis=-1, keepdims=True) + NORM_EPS)
    resid[...] = residual
    pooled = jnp.sum(residual * inv_rms * gain, axis=0, keepdims=True) / rows
    pooled = pooled.astype(jnp.bfloat16).astype(jnp.float32)
    pool_mine[...] = pooled
    pool_all[pl.ds(expert, 1)] = pooled[None]

    def small(i, src, dst, off):
        return pltpu.make_async_remote_copy(
            src_ref=src,
            dst_ref=dst,
            send_sem=small_send.at[i, off],
            recv_sem=small_recv.at[i, off],
            device_id={"expert": lax.rem(expert + off, n)},
        )

    copies = [small(0, pool_mine, pool_all.at[expert], off) for off in range(1, n)]
    for copy in copies:
        copy.start()
    for copy in copies:
        copy.wait()
    pooled_rows = jnp.concatenate([pool_all[i] for i in range(n)], axis=0).astype(jnp.bfloat16)
    logits = jnp.dot(pooled_rows, head_ref[...], preferred_element_type=jnp.float32)
    sig = 1.0 / (1.0 + jnp.exp(-logits))
    logit_grad = (LOSS_SCALE * (sig - target_ref[...].astype(jnp.float32))).astype(jnp.bfloat16)
    pooled_terms = lax.dot_general(logit_grad, head_ref[...], NT, preferred_element_type=jnp.float32)
    for i in range(n):
        terms[i] = pooled_terms[i : i + 1, :]
    copies = [
        small(1, terms.at[lax.rem(expert + off, n)], terms_in.at[off], off) for off in range(1, n)
    ]
    for copy in copies:
        copy.start()
    pool_ref[pl.ds(group, 1)] = pooled_rows.astype(jnp.float32)[None]
    lg_ref[pl.ds(group, 1)] = logit_grad.astype(jnp.float32)[None]
    group_copies = []
    for off in range(1, groups):
        for i, ref in enumerate((pool_ref, lg_ref)):
            copy = pltpu.make_async_remote_copy(
                src_ref=ref.at[group],
                dst_ref=ref.at[group],
                send_sem=group_send.at[off, i],
                recv_sem=group_recv.at[off, i],
                device_id={"group": lax.rem(group + off, groups)},
            )
            copy.start()
            group_copies.append(copy)
    for copy in copies:
        copy.wait()
    pooled_grad = terms[expert]
    for off in range(1, n):
        pooled_grad = pooled_grad + terms_in[off]
    residual = resid[...]
    inv_rms = lax.rsqrt(jnp.mean(residual * residual, axis=-1, keepdims=True) + NORM_EPS)
    scaled = gain * pooled_grad / rows
    cube = inv_rms * inv_rms * inv_rms
    resid_grad = inv_rms * scaled - residual * (
        cube * jnp.mean(residual * scaled, axis=-1, keepdims=True)
    )
    gbuf[0] = resid_grad.astype(jnp.bfloat16)
    for c in range(pieces):
        cw(gbuf, 1, 0, c).start()
        ccw(gbuf, 1, n, c).start()
    resid[...] = resid_grad
    gather_phase(gbuf, 1, backward_block, lambda: None)
    out_ref[...] = (resid[...] + reduce_phase(1)).astype(jnp.bfloat16)
    for copy in group_copies:
        copy.wait()


def body(tokens, w_gate, w_up, w_down, route_ids, route_scores, norm_gain, class_head, targets):
    rows, width = tokens.shape
    n = lax.axis_size("expert")
    groups = lax.axis_size("group")
    local, _, hidden = w_gate.shape
    labels = class_head.shape[1]
    half = n // 2
    gather_weights = w_gate.shape[1] % 16 == 0 and w_down.shape[1] % 16 == 0
    if not gather_weights:
        w_gate = lax.all_gather(w_gate, "group", axis=1, tiled=True)
        w_up = lax.all_gather(w_up, "group", axis=1, tiled=True)
        w_down = lax.all_gather(w_down, "group", axis=1, tiled=True)
    vmem = pl.BlockSpec(memory_space=pltpu.VMEM)
    hbm = pl.BlockSpec(memory_space=pl.ANY)
    dma = pltpu.SemaphoreType.DMA
    bf16, f32 = jnp.bfloat16, jnp.float32
    token_grad, pool, lg = pl.pallas_call(
        functools.partial(kernel, n, groups, gather_weights, n == 8),
        out_shape=(
            jax.ShapeDtypeStruct((rows, width), bf16),
            jax.ShapeDtypeStruct((groups, n, width), f32),
            jax.ShapeDtypeStruct((groups, n, labels), f32),
        ),
        in_specs=[vmem] * 6 + [hbm] * 3,
        out_specs=(vmem, vmem, vmem),
        scratch_shapes=[
            pltpu.VMEM((local, width, hidden), bf16),
            pltpu.VMEM((local, width, hidden), bf16),
            pltpu.VMEM((local, hidden, width), bf16),
            pltpu.VMEM((n, rows, width + LANES), bf16),
            pltpu.VMEM((n, rows, width), bf16),
            pltpu.VMEM((n, local, rows, hidden), f32),
            pltpu.VMEM((n, local, rows, hidden), f32),
            pltpu.VMEM((2, n, rows, width), bf16),
            pltpu.VMEM((2, half, rows, width), bf16),
            pltpu.VMEM((2, half, rows, width), bf16),
            pltpu.VMEM((rows, width), f32),
            pltpu.VMEM((1, width), f32),
            pltpu.VMEM((n, 1, width), f32),
            pltpu.VMEM((n, 1, width), f32),
            pltpu.VMEM((n, 1, width), f32),
            dma((3,)),
            dma((groups, 3)),
            dma((groups, 3)),
            dma((2, 4, n)),
            dma((2, 4, n)),
            dma((2, 4, n)),
            dma((2, 4, n)),
            dma((2, 4, n)),
            dma((2, 4, n)),
            dma((2, 4, n)),
            dma((2, n)),
            dma((2, n)),
            dma((groups, 2)),
            dma((groups, 2)),
        ],
        compiler_params=pltpu.CompilerParams(
            collective_id=0, has_side_effects=True, vmem_limit_bytes=60 * 1024 * 1024
        ),
    )(
        tokens,
        route_ids,
        route_scores,
        norm_gain.reshape(1, width),
        class_head,
        targets.reshape(n, labels),
        w_gate,
        w_up,
        w_down,
    )
    head_grad = lax.dot_general(
        pool.reshape(-1, width).astype(bf16),
        lg.reshape(-1, labels).astype(bf16),
        (((0,), (0,)), ((), ())),
        preferred_element_type=f32,
    )
    return token_grad, head_grad


def solution(mesh):
    in_specs = (
        P(("rep", "expert", "group"), None),
        P("expert", "group", None),
        P("expert", "group", None),
        P("expert", "group", None),
        P(("rep", "expert", "group"), None),
        P(("rep", "expert", "group"), None),
        P(),
        P(None, "expert"),
        P("rep", "group", "expert"),
    )
    out_specs = (P(("rep", "expert", "group"), None), P("rep", "expert"))
    return jax.shard_map(body, mesh=mesh, in_specs=in_specs, out_specs=out_specs, check_vma=False)
```

```python
import functools

import jax
import jax.numpy as jnp
from jax import lax
from jax.experimental import pallas as pl
from jax.experimental.pallas import tpu as pltpu
from jax.sharding import PartitionSpec as P

LOSS_SCALE = 8.0
NORM_EPS = 1e-06
LANES = 128
HALF = 64
NT = (((1,), (1,)), ((), ()))


def ring_place(expert, n, snake):
    if not snake:
        return expert
    odd = lax.rem(expert, 2)
    return (1 - odd) * (expert // 2) + odd * (n - 1 - expert // 2)


def ring_expert(place, n, snake):
    if not snake:
        return place
    back = place // (n // 2)
    return (1 - back) * 2 * place + back * (2 * n - 1 - 2 * place)


def kernel(
    n,
    groups,
    gather_weights,
    snake,
    tok_ref,
    ids_ref,
    score_ref,
    gain_ref,
    head_ref,
    target_ref,
    wg_ref,
    wu_ref,
    wd_ref,
    out_ref,
    pool_ref,
    lg_ref,
    wg,
    wu,
    wd,
    xbuf,
    gbuf,
    gate_coef,
    up_coef,
    part,
    from_right,
    from_left,
    resid,
    pool_mine,
    pool_all,
    terms,
    terms_in,
    grad_mine,
    pool_grads,
    w_local_sem,
    w_send_sem,
    w_recv_sem,
    cw_send,
    ccw_send,
    ring_recv,
    left_send,
    right_send,
    left_recv,
    right_recv,
    small_send,
    small_recv,
    group_send,
    group_recv,
):
    rows, width = tok_ref.shape
    local, _, hidden = wg.shape
    half = n // 2
    expert = lax.axis_index("expert")
    group = lax.axis_index("group")
    place = ring_place(expert, n, snake)
    right = ring_expert(lax.rem(place + 1, n), n, snake)
    left = ring_expert(lax.rem(place + n - 1, n), n, snake)

    barrier = pltpu.get_barrier_semaphore()
    for off in range(1, n):
        pl.semaphore_signal(barrier, inc=1, device_id={"expert": lax.rem(expert + off, n)})
    for off in range(1, groups):
        pl.semaphore_signal(barrier, inc=1, device_id={"group": lax.rem(group + off, groups)})

    locals_ = []
    for i, (src, dst) in enumerate(((wg_ref, wg), (wu_ref, wu), (wd_ref, wd))):
        span = src.shape[1]
        at = pl.multiple_of(group * span, 16) if gather_weights else 0
        copy = pltpu.make_async_copy(src, dst.at[:, pl.ds(at, span), :], w_local_sem.at[i])
        copy.start()
        locals_.append(copy)

    ids = ids_ref[...]
    score = score_ref[...]
    weight = score / jnp.sum(score, axis=-1, keepdims=True)
    lane = lax.rem(lax.broadcasted_iota(jnp.int32, (rows, LANES), 1), HALF)
    low = lax.broadcasted_iota(jnp.int32, (rows, LANES), 1) < HALF
    by_expert = jnp.zeros((rows, LANES), jnp.float32)
    for k in range(ids.shape[1]):
        by_expert += jnp.where(lane == ids[:, k : k + 1], weight[:, k : k + 1], 0.0)
    high_part = by_expert.astype(jnp.bfloat16).astype(jnp.float32)
    xbuf[0, :, :width] = tok_ref[...]
    xbuf[0, :, width:] = jnp.where(low, high_part, by_expert - high_part).astype(jnp.bfloat16)

    pl.semaphore_wait(barrier, n - 1 + groups - 1)

    pieces = 4
    piece = rows // pieces
    turn = pieces // 2

    def chunk(buf, at, c):
        return buf.at[(*at, pl.ds(c * piece, piece))]

    def cw(buf, phase, k, c):
        return pltpu.make_async_remote_copy(
            src_ref=chunk(buf, (k,), c),
            dst_ref=chunk(buf, (k + 1,), c),
            send_sem=cw_send.at[phase, c, k],
            recv_sem=ring_recv.at[phase, c, k + 1],
            device_id={"expert": right},
        )

    def ccw(buf, phase, k, c):
        return pltpu.make_async_remote_copy(
            src_ref=chunk(buf, (lax.rem(k, n),), c),
            dst_ref=chunk(buf, (k - 1,), c),
            send_sem=ccw_send.at[phase, c, k - 1],
            recv_sem=ring_recv.at[phase, c, k - 1],
            device_id={"expert": left},
        )

    for c in range(pieces):
        cw(xbuf, 0, 0, c).start()
        ccw(xbuf, 0, n, c).start()

    w_copies = []
    if gather_weights:
        for off in range(1, groups):
            for i, (src, dst) in enumerate(((wg_ref, wg), (wu_ref, wu), (wd_ref, wd))):
                span = src.shape[1]
                at = pl.multiple_of(group * span, 16)
                copy = pltpu.make_async_remote_copy(
                    src_ref=src,
                    dst_ref=dst.at[:, pl.ds(at, span), :],
                    send_sem=w_send_sem.at[off, i],
                    recv_sem=w_recv_sem.at[off, i],
                    device_id={"group": lax.rem(group + off, groups)},
                )
                copy.start()
                w_copies.append(copy)

    def weights_ready():
        for copy in locals_:
            copy.wait()
        for copy in w_copies:
            copy.wait()

    def forward_block(k):
        x = xbuf[k, :, :width]
        ext = xbuf[k, :, width:].astype(jnp.float32)
        total = jnp.zeros((rows, width), jnp.float32)
        for j in range(local):
            w = jnp.sum(jnp.where(lane == expert * local + j, ext, 0.0), axis=1, keepdims=True)
            gate = jnp.dot(x, wg[j], preferred_element_type=jnp.float32)
            up = jnp.dot(x, wu[j], preferred_element_type=jnp.float32)
            sig = 1.0 / (1.0 + jnp.exp(-gate))
            silu = gate * sig * w
            gate_coef[k, j] = up * (sig * (1.0 + gate * (1.0 - sig))) * w
            up_coef[k, j] = silu
            total += jnp.dot(
                (silu * up).astype(jnp.bfloat16), wd[j], preferred_element_type=jnp.float32
            )
        part[0, k] = total.astype(jnp.bfloat16)

    def residual_gradient(residual, pooled_grad):
        inv_rms = lax.rsqrt(jnp.mean(residual * residual, axis=-1, keepdims=True) + NORM_EPS)
        scaled = gain_ref[...] * pooled_grad / rows
        cube = inv_rms * inv_rms * inv_rms
        return inv_rms * scaled - residual * (
            cube * jnp.mean(residual * scaled, axis=-1, keepdims=True)
        )

    def backward_block(k):
        source = ring_expert(lax.rem(place - k + n, n), n, snake)
        g = residual_gradient(gbuf[k].astype(jnp.float32), pool_grads[source]).astype(jnp.bfloat16)
        total = jnp.zeros((rows, width), jnp.float32)
        for j in range(local):
            back = lax.dot_general(g, wd[j], NT, preferred_element_type=jnp.float32)
            gate_grad = (back * gate_coef[k, j]).astype(jnp.bfloat16)
            up_grad = (back * up_coef[k, j]).astype(jnp.bfloat16)
            total += lax.dot_general(gate_grad, wg[j], NT, preferred_element_type=jnp.float32)
            total += lax.dot_general(up_grad, wu[j], NT, preferred_element_type=jnp.float32)
        part[1, k] = total.astype(jnp.bfloat16)

    def gather_phase(buf, phase, block, ready):
        def arrive(s):
            for c in range(pieces):
                cw(buf, phase, s - 1, c).wait_recv()

                @pl.when((s < half - 1) | (c < turn))
                def _():
                    cw(buf, phase, s, c).start()

                ccw(buf, phase, n - s + 1, c).wait_recv()

                @pl.when((s < half - 1) | (c >= turn))
                def _():
                    ccw(buf, phase, n - s, c).start()

        lead = len(ready) - 1
        for at, action in enumerate(ready):
            arrive(jnp.int32(at + 1))
            action()

        def step(i, carry):
            s = (i + 1) // 2
            odd = lax.rem(i, 2)

            @pl.when((odd == 1) & (s > 1) & (s + lead < half))
            def _():
                arrive(s + lead)

            @pl.when((odd == 1) & (s == half))
            def _():
                for c in range(turn):
                    cw(buf, phase, half - 1, c).wait_recv()
                    ccw(buf, phase, half + 1, c + turn).wait_recv()

            block(odd * s + (1 - odd) * lax.rem(n - s, n))
            return carry

        lax.fori_loop(0, n, step, 0)
        for c in range(pieces):

            def drain_cw(k, carry):
                cw(buf, phase, k, c).wait_send()
                return carry

            def drain_ccw(k, carry):
                ccw(buf, phase, n - k, c).wait_send()
                return carry

            lax.fori_loop(0, half - c // turn, drain_cw, 0)
            lax.fori_loop(0, half - 1 + c // turn, drain_ccw, 0)

    def to_left(phase, k, c):
        return pltpu.make_async_remote_copy(
            src_ref=chunk(part, (phase, k), c),
            dst_ref=chunk(from_right, (phase, k - 1), c),
            send_sem=left_send.at[phase, c, k],
            recv_sem=left_recv.at[phase, c, k - 1],
            device_id={"expert": left},
        )

    def to_right(phase, d, c):
        return pltpu.make_async_remote_copy(
            src_ref=chunk(part, (phase, n - d), c),
            dst_ref=chunk(from_left, (phase, d - 1), c),
            send_sem=right_send.at[phase, c, d],
            recv_sem=right_recv.at[phase, c, d - 1],
            device_id={"expert": right},
        )

    def add_piece(phase, slot, incoming, at, c):
        span = pl.ds(c * piece, piece)
        part[phase, slot, span] = (
            part[phase, slot, span].astype(jnp.float32)
            + incoming[phase, at, span].astype(jnp.float32)
        ).astype(jnp.bfloat16)

    def reduce_phase(phase):
        for c in range(turn):
            to_left(phase, half, c).start()
            to_right(phase, half, c + turn).start()
        for c in range(turn):
            to_right(phase, half - 1, c).start()
            to_left(phase, half - 1, c + turn).start()

        def pass_left(k, c):
            to_left(phase, k + 1, c).wait_recv()
            add_piece(phase, k, from_right, k, c)
            to_left(phase, k, c).start()

        def pass_right(d, c):
            to_right(phase, d + 1, c).wait_recv()
            add_piece(phase, n - d, from_left, d, c)
            to_right(phase, d, c).start()

        def step(s, carry):
            for c in range(turn):
                pass_left(half - s, c)
                pass_right(half - s, c + turn)

            @pl.when(s < half - 1)
            def _():
                for c in range(turn):
                    pass_right(half - 1 - s, c)
                    pass_left(half - 1 - s, c + turn)

            return carry

        lax.fori_loop(1, half, step, 0)
        for c in range(pieces):
            to_right(phase, 1, c).wait_recv()
            to_left(phase, 1, c).wait_recv()

            def drain_left(k, carry):
                to_left(phase, k, c).wait_send()
                return carry

            def drain_right(d, carry):
                to_right(phase, d, c).wait_send()
                return carry

            lax.fori_loop(1, half + 1 - c // turn, drain_left, 0)
            lax.fori_loop(1, half + c // turn, drain_right, 0)
        return (
            part[phase, 0].astype(jnp.float32)
            + from_right[phase, 0].astype(jnp.float32)
            + from_left[phase, 0].astype(jnp.float32)
        )

    gather_phase(xbuf, 0, forward_block, [weights_ready])
    residual = xbuf[0, :, :width].astype(jnp.float32) + reduce_phase(0)
    gain = gain_ref[...]
    inv_rms = lax.rsqrt(jnp.mean(residual * residual, axis=-1, keepdims=True) + NORM_EPS)
    resid[...] = residual
    gbuf[0] = residual.astype(jnp.bfloat16)
    pooled = jnp.sum(residual * inv_rms * gain, axis=0, keepdims=True) / rows
    pooled = pooled.astype(jnp.bfloat16).astype(jnp.float32)
    pool_mine[...] = pooled
    pool_all[pl.ds(expert, 1)] = pooled[None]

    def small(i, src, dst, off):
        return pltpu.make_async_remote_copy(
            src_ref=src,
            dst_ref=dst,
            send_sem=small_send.at[i, off],
            recv_sem=small_recv.at[i, off],
            device_id={"expert": lax.rem(expert + off, n)},
        )

    copies = [small(0, pool_mine, pool_all.at[expert], off) for off in range(1, n)]
    for copy in copies:
        copy.start()
    for c in range(pieces):
        cw(gbuf, 1, 0, c).start()
        ccw(gbuf, 1, n, c).start()
    for copy in copies:
        copy.wait()
    pooled_rows = jnp.concatenate([pool_all[i] for i in range(n)], axis=0).astype(jnp.bfloat16)
    logits = jnp.dot(pooled_rows, head_ref[...], preferred_element_type=jnp.float32)
    sig = 1.0 / (1.0 + jnp.exp(-logits))
    logit_grad = (LOSS_SCALE * (sig - target_ref[...].astype(jnp.float32))).astype(jnp.bfloat16)
    pooled_terms = lax.dot_general(logit_grad, head_ref[...], NT, preferred_element_type=jnp.float32)
    for i in range(n):
        terms[i] = pooled_terms[i : i + 1, :]
    copies = [
        small(1, terms.at[lax.rem(expert + off, n)], terms_in.at[off], off) for off in range(1, n)
    ]
    for copy in copies:
        copy.start()
    pool_ref[pl.ds(group, 1)] = pooled_rows.astype(jnp.float32)[None]
    lg_ref[pl.ds(group, 1)] = logit_grad.astype(jnp.float32)[None]
    group_copies = []
    for off in range(1, groups):
        for i, ref in enumerate((pool_ref, lg_ref)):
            copy = pltpu.make_async_remote_copy(
                src_ref=ref.at[group],
                dst_ref=ref.at[group],
                send_sem=group_send.at[off, i],
                recv_sem=group_recv.at[off, i],
                device_id={"group": lax.rem(group + off, groups)},
            )
            copy.start()
            group_copies.append(copy)
    grad_copies = [small(2, grad_mine, pool_grads.at[expert], off) for off in range(1, n)]

    def send_pooled_grad():
        for copy in copies:
            copy.wait()
        pooled_grad = terms[expert]
        for off in range(1, n):
            pooled_grad = pooled_grad + terms_in[off]
        grad_mine[...] = pooled_grad
        pool_grads[pl.ds(expert, 1)] = pooled_grad[None]
        for copy in grad_copies:
            copy.start()
        resid[...] = residual_gradient(resid[...], pooled_grad)

    def pooled_grads_ready():
        for copy in grad_copies:
            copy.wait()

    gather_phase(gbuf, 1, backward_block, [send_pooled_grad, pooled_grads_ready])
    out_ref[...] = (resid[...] + reduce_phase(1)).astype(jnp.bfloat16)
    for copy in group_copies:
        copy.wait()


def body(tokens, w_gate, w_up, w_down, route_ids, route_scores, norm_gain, class_head, targets):
    rows, width = tokens.shape
    n = lax.axis_size("expert")
    groups = lax.axis_size("group")
    local, _, hidden = w_gate.shape
    labels = class_head.shape[1]
    half = n // 2
    gather_weights = w_gate.shape[1] % 16 == 0 and w_down.shape[1] % 16 == 0
    if not gather_weights:
        w_gate = lax.all_gather(w_gate, "group", axis=1, tiled=True)
        w_up = lax.all_gather(w_up, "group", axis=1, tiled=True)
        w_down = lax.all_gather(w_down, "group", axis=1, tiled=True)
    vmem = pl.BlockSpec(memory_space=pltpu.VMEM)
    hbm = pl.BlockSpec(memory_space=pl.ANY)
    dma = pltpu.SemaphoreType.DMA
    bf16, f32 = jnp.bfloat16, jnp.float32
    token_grad, pool, lg = pl.pallas_call(
        functools.partial(kernel, n, groups, gather_weights, n == 8),
        out_shape=(
            jax.ShapeDtypeStruct((rows, width), bf16),
            jax.ShapeDtypeStruct((groups, n, width), f32),
            jax.ShapeDtypeStruct((groups, n, labels), f32),
        ),
        in_specs=[vmem] * 6 + [hbm] * 3,
        out_specs=(vmem, vmem, vmem),
        scratch_shapes=[
            pltpu.VMEM((local, width, hidden), bf16),
            pltpu.VMEM((local, width, hidden), bf16),
            pltpu.VMEM((local, hidden, width), bf16),
            pltpu.VMEM((n, rows, width + LANES), bf16),
            pltpu.VMEM((n, rows, width), bf16),
            pltpu.VMEM((n, local, rows, hidden), f32),
            pltpu.VMEM((n, local, rows, hidden), f32),
            pltpu.VMEM((2, n, rows, width), bf16),
            pltpu.VMEM((2, half, rows, width), bf16),
            pltpu.VMEM((2, half, rows, width), bf16),
            pltpu.VMEM((rows, width), f32),
            pltpu.VMEM((1, width), f32),
            pltpu.VMEM((n, 1, width), f32),
            pltpu.VMEM((n, 1, width), f32),
            pltpu.VMEM((n, 1, width), f32),
            pltpu.VMEM((1, width), f32),
            pltpu.VMEM((n, 1, width), f32),
            dma((3,)),
            dma((groups, 3)),
            dma((groups, 3)),
            dma((2, 4, n)),
            dma((2, 4, n)),
            dma((2, 4, n)),
            dma((2, 4, n)),
            dma((2, 4, n)),
            dma((2, 4, n)),
            dma((2, 4, n)),
            dma((3, n)),
            dma((3, n)),
            dma((groups, 2)),
            dma((groups, 2)),
        ],
        compiler_params=pltpu.CompilerParams(
            collective_id=0, has_side_effects=True, vmem_limit_bytes=60 * 1024 * 1024
        ),
    )(
        tokens,
        route_ids,
        route_scores,
        norm_gain.reshape(1, width),
        class_head,
        targets.reshape(n, labels),
        w_gate,
        w_up,
        w_down,
    )
    head_grad = lax.dot_general(
        pool.reshape(-1, width).astype(bf16),
        lg.reshape(-1, labels).astype(bf16),
        (((0,), (0,)), ((), ())),
        preferred_element_type=f32,
    )
    return token_grad, head_grad


def solution(mesh):
    in_specs = (
        P(("rep", "expert", "group"), None),
        P("expert", "group", None),
        P("expert", "group", None),
        P("expert", "group", None),
        P(("rep", "expert", "group"), None),
        P(("rep", "expert", "group"), None),
        P(),
        P(None, "expert"),
        P("rep", "group", "expert"),
    )
    out_specs = (P(("rep", "expert", "group"), None), P("rep", "expert"))
    return jax.shard_map(body, mesh=mesh, in_specs=in_specs, out_specs=out_specs, check_vma=False)
```

```python
import functools

import jax
import jax.numpy as jnp
from jax import lax
from jax.experimental import pallas as pl
from jax.experimental.pallas import tpu as pltpu
from jax.sharding import PartitionSpec as P

LOSS_SCALE = 8.0
NORM_EPS = 1e-06
LANES = 128
HALF = 64
NT = (((1,), (1,)), ((), ()))


def ring_place(expert, n, snake):
    if not snake:
        return expert
    odd = lax.rem(expert, 2)
    return (1 - odd) * (expert // 2) + odd * (n - 1 - expert // 2)


def ring_expert(place, n, snake):
    if not snake:
        return place
    back = place // (n // 2)
    return (1 - back) * 2 * place + back * (2 * n - 1 - 2 * place)


def kernel(
    n,
    groups,
    gather_weights,
    snake,
    tok_ref,
    ids_ref,
    score_ref,
    gain_ref,
    head_ref,
    target_ref,
    wg_ref,
    wu_ref,
    wd_ref,
    out_ref,
    pool_ref,
    lg_ref,
    wg,
    wu,
    wd,
    xbuf,
    gbuf,
    gate_coef,
    up_coef,
    part,
    from_right,
    from_left,
    resid,
    pool_mine,
    pool_all,
    terms,
    terms_in,
    grad_mine,
    pool_grads,
    w_local_sem,
    w_send_sem,
    w_recv_sem,
    cw_send,
    ccw_send,
    ring_recv,
    left_send,
    right_send,
    left_recv,
    right_recv,
    small_send,
    small_recv,
    group_send,
    group_recv,
):
    rows, width = tok_ref.shape
    local, _, hidden = wg.shape
    half = n // 2
    expert = lax.axis_index("expert")
    group = lax.axis_index("group")
    place = ring_place(expert, n, snake)
    right = ring_expert(lax.rem(place + 1, n), n, snake)
    left = ring_expert(lax.rem(place + n - 1, n), n, snake)

    barrier = pltpu.get_barrier_semaphore()
    for off in range(1, n):
        pl.semaphore_signal(barrier, inc=1, device_id={"expert": lax.rem(expert + off, n)})
    for off in range(1, groups):
        pl.semaphore_signal(barrier, inc=1, device_id={"group": lax.rem(group + off, groups)})

    locals_ = []
    for i, (src, dst) in enumerate(((wg_ref, wg), (wu_ref, wu), (wd_ref, wd))):
        span = src.shape[1]
        at = pl.multiple_of(group * span, 16) if gather_weights else 0
        copy = pltpu.make_async_copy(src, dst.at[:, pl.ds(at, span), :], w_local_sem.at[i])
        copy.start()
        locals_.append(copy)

    ids = ids_ref[...]
    score = score_ref[...]
    weight = score / jnp.sum(score, axis=0, keepdims=True)
    lane = lax.rem(lax.broadcasted_iota(jnp.int32, (rows, LANES), 1), HALF)
    low = lax.broadcasted_iota(jnp.int32, (rows, LANES), 1) < HALF
    named = lax.rem(lax.broadcasted_iota(jnp.int32, (LANES, rows), 0), HALF)
    by_expert = jnp.zeros((LANES, rows), jnp.float32)
    for k in range(ids.shape[0]):
        by_expert += jnp.where(named == ids[k : k + 1, :], weight[k : k + 1, :], 0.0)
    by_expert = by_expert.T
    high_part = by_expert.astype(jnp.bfloat16).astype(jnp.float32)
    xbuf[0, :, :width] = tok_ref[...]
    xbuf[0, :, width:] = jnp.where(low, high_part, by_expert - high_part).astype(jnp.bfloat16)

    pl.semaphore_wait(barrier, n - 1 + groups - 1)

    pieces = 4
    piece = rows // pieces
    turn = pieces // 2

    def chunk(buf, at, c):
        return buf.at[(*at, pl.ds(c * piece, piece))]

    def cw(buf, phase, k, c):
        return pltpu.make_async_remote_copy(
            src_ref=chunk(buf, (k,), c),
            dst_ref=chunk(buf, (k + 1,), c),
            send_sem=cw_send.at[phase, c, k],
            recv_sem=ring_recv.at[phase, c, k + 1],
            device_id={"expert": right},
        )

    def ccw(buf, phase, k, c):
        return pltpu.make_async_remote_copy(
            src_ref=chunk(buf, (lax.rem(k, n),), c),
            dst_ref=chunk(buf, (k - 1,), c),
            send_sem=ccw_send.at[phase, c, k - 1],
            recv_sem=ring_recv.at[phase, c, k - 1],
            device_id={"expert": left},
        )

    for c in range(pieces):
        cw(xbuf, 0, 0, c).start()
        ccw(xbuf, 0, n, c).start()

    w_copies = []
    if gather_weights:
        for off in range(1, groups):
            for i, (src, dst) in enumerate(((wg_ref, wg), (wu_ref, wu), (wd_ref, wd))):
                span = src.shape[1]
                at = pl.multiple_of(group * span, 16)
                copy = pltpu.make_async_remote_copy(
                    src_ref=src,
                    dst_ref=dst.at[:, pl.ds(at, span), :],
                    send_sem=w_send_sem.at[off, i],
                    recv_sem=w_recv_sem.at[off, i],
                    device_id={"group": lax.rem(group + off, groups)},
                )
                copy.start()
                w_copies.append(copy)

    def weights_ready():
        for copy in locals_:
            copy.wait()
        for copy in w_copies:
            copy.wait()

    def forward_block(k):
        x = xbuf[k, :, :width]
        ext = xbuf[k, :, width:].astype(jnp.float32)
        total = jnp.zeros((rows, width), jnp.float32)
        for j in range(local):
            w = jnp.sum(jnp.where(lane == expert * local + j, ext, 0.0), axis=1, keepdims=True)
            gate = jnp.dot(x, wg[j], preferred_element_type=jnp.float32)
            up = jnp.dot(x, wu[j], preferred_element_type=jnp.float32)
            sig = 1.0 / (1.0 + jnp.exp(-gate))
            silu = gate * sig * w
            gate_coef[k, j] = up * (sig * (1.0 + gate * (1.0 - sig))) * w
            up_coef[k, j] = silu
            total += jnp.dot(
                (silu * up).astype(jnp.bfloat16), wd[j], preferred_element_type=jnp.float32
            )
        part[0, k] = total.astype(jnp.bfloat16)

    def residual_gradient(residual, pooled_grad):
        inv_rms = lax.rsqrt(jnp.mean(residual * residual, axis=-1, keepdims=True) + NORM_EPS)
        scaled = gain_ref[...] * pooled_grad / rows
        cube = inv_rms * inv_rms * inv_rms
        return inv_rms * scaled - residual * (
            cube * jnp.mean(residual * scaled, axis=-1, keepdims=True)
        )

    def backward_block(k):
        source = ring_expert(lax.rem(place - k + n, n), n, snake)
        g = residual_gradient(gbuf[k].astype(jnp.float32), pool_grads[source]).astype(jnp.bfloat16)
        total = jnp.zeros((rows, width), jnp.float32)
        for j in range(local):
            back = lax.dot_general(g, wd[j], NT, preferred_element_type=jnp.float32)
            gate_grad = (back * gate_coef[k, j]).astype(jnp.bfloat16)
            up_grad = (back * up_coef[k, j]).astype(jnp.bfloat16)
            total += lax.dot_general(gate_grad, wg[j], NT, preferred_element_type=jnp.float32)
            total += lax.dot_general(up_grad, wu[j], NT, preferred_element_type=jnp.float32)
        part[1, k] = total.astype(jnp.bfloat16)

    def gather_phase(buf, phase, block, ready):
        def arrive(s):
            for c in range(pieces):
                cw(buf, phase, s - 1, c).wait_recv()

                @pl.when((s < half - 1) | (c < turn))
                def _():
                    cw(buf, phase, s, c).start()

                ccw(buf, phase, n - s + 1, c).wait_recv()

                @pl.when((s < half - 1) | (c >= turn))
                def _():
                    ccw(buf, phase, n - s, c).start()

        lead = len(ready) - 1
        for at, action in enumerate(ready):
            arrive(jnp.int32(at + 1))
            action()

        def step(i, carry):
            s = (i + 1) // 2
            odd = lax.rem(i, 2)

            @pl.when((odd == 1) & (s > 1) & (s + lead < half))
            def _():
                arrive(s + lead)

            @pl.when((odd == 1) & (s == half))
            def _():
                for c in range(turn):
                    cw(buf, phase, half - 1, c).wait_recv()
                    ccw(buf, phase, half + 1, c + turn).wait_recv()

            block(odd * s + (1 - odd) * lax.rem(n - s, n))

            @pl.when(i == n - 2)
            def _():
                for c in range(turn):
                    to_right(phase, half - 1, c).start()
                    to_left(phase, half - 1, c + turn).start()

            return carry

        lax.fori_loop(0, n, step, 0)
        for c in range(pieces):

            def drain_cw(k, carry):
                cw(buf, phase, k, c).wait_send()
                return carry

            def drain_ccw(k, carry):
                ccw(buf, phase, n - k, c).wait_send()
                return carry

            lax.fori_loop(0, half - c // turn, drain_cw, 0)
            lax.fori_loop(0, half - 1 + c // turn, drain_ccw, 0)

    def to_left(phase, k, c):
        return pltpu.make_async_remote_copy(
            src_ref=chunk(part, (phase, k), c),
            dst_ref=chunk(from_right, (phase, k - 1), c),
            send_sem=left_send.at[phase, c, k],
            recv_sem=left_recv.at[phase, c, k - 1],
            device_id={"expert": left},
        )

    def to_right(phase, d, c):
        return pltpu.make_async_remote_copy(
            src_ref=chunk(part, (phase, n - d), c),
            dst_ref=chunk(from_left, (phase, d - 1), c),
            send_sem=right_send.at[phase, c, d],
            recv_sem=right_recv.at[phase, c, d - 1],
            device_id={"expert": right},
        )

    def add_piece(phase, slot, incoming, at, c):
        span = pl.ds(c * piece, piece)
        part[phase, slot, span] = (
            part[phase, slot, span].astype(jnp.float32)
            + incoming[phase, at, span].astype(jnp.float32)
        ).astype(jnp.bfloat16)

    def reduce_phase(phase):
        for c in range(turn):
            to_left(phase, half, c).start()
            to_right(phase, half, c + turn).start()

        def pass_left(k, c):
            to_left(phase, k + 1, c).wait_recv()
            add_piece(phase, k, from_right, k, c)
            to_left(phase, k, c).start()

        def pass_right(d, c):
            to_right(phase, d + 1, c).wait_recv()
            add_piece(phase, n - d, from_left, d, c)
            to_right(phase, d, c).start()

        def step(s, carry):
            for c in range(turn):
                pass_left(half - s, c)
                pass_right(half - s, c + turn)

            @pl.when(s < half - 1)
            def _():
                for c in range(turn):
                    pass_right(half - 1 - s, c)
                    pass_left(half - 1 - s, c + turn)

            return carry

        lax.fori_loop(1, half, step, 0)
        for c in range(pieces):
            to_right(phase, 1, c).wait_recv()
            to_left(phase, 1, c).wait_recv()

            def drain_left(k, carry):
                to_left(phase, k, c).wait_send()
                return carry

            def drain_right(d, carry):
                to_right(phase, d, c).wait_send()
                return carry

            lax.fori_loop(1, half + 1 - c // turn, drain_left, 0)
            lax.fori_loop(1, half + c // turn, drain_right, 0)
        return (
            part[phase, 0].astype(jnp.float32)
            + from_right[phase, 0].astype(jnp.float32)
            + from_left[phase, 0].astype(jnp.float32)
        )

    gather_phase(xbuf, 0, forward_block, [weights_ready])
    residual = xbuf[0, :, :width].astype(jnp.float32) + reduce_phase(0)
    gain = gain_ref[...]
    inv_rms = lax.rsqrt(jnp.mean(residual * residual, axis=-1, keepdims=True) + NORM_EPS)
    resid[...] = residual
    gbuf[0] = residual.astype(jnp.bfloat16)
    pooled = jnp.sum(residual * inv_rms * gain, axis=0, keepdims=True) / rows
    pooled = pooled.astype(jnp.bfloat16).astype(jnp.float32)
    pool_mine[...] = pooled
    pool_all[pl.ds(expert, 1)] = pooled[None]

    def small(i, src, dst, off):
        return pltpu.make_async_remote_copy(
            src_ref=src,
            dst_ref=dst,
            send_sem=small_send.at[i, off],
            recv_sem=small_recv.at[i, off],
            device_id={"expert": lax.rem(expert + off, n)},
        )

    copies = [small(0, pool_mine, pool_all.at[expert], off) for off in range(1, n)]
    for copy in copies:
        copy.start()
    for c in range(pieces):
        cw(gbuf, 1, 0, c).start()
        ccw(gbuf, 1, n, c).start()
    for copy in copies:
        copy.wait()
    pooled_rows = jnp.concatenate([pool_all[i] for i in range(n)], axis=0).astype(jnp.bfloat16)
    logits = jnp.dot(pooled_rows, head_ref[...], preferred_element_type=jnp.float32)
    target_rows = jnp.concatenate([target_ref[i] for i in range(n)], axis=0)
    sig = 1.0 / (1.0 + jnp.exp(-logits))
    logit_grad = (LOSS_SCALE * (sig - target_rows.astype(jnp.float32))).astype(jnp.bfloat16)
    pooled_terms = lax.dot_general(logit_grad, head_ref[...], NT, preferred_element_type=jnp.float32)
    for i in range(n):
        terms[i] = pooled_terms[i : i + 1, :]
    copies = [
        small(1, terms.at[lax.rem(expert + off, n)], terms_in.at[off], off) for off in range(1, n)
    ]
    for copy in copies:
        copy.start()
    pool_ref[pl.ds(group, 1)] = pooled_rows.astype(jnp.float32)[None]
    lg_ref[pl.ds(group, 1)] = logit_grad.astype(jnp.float32)[None]
    group_copies = []
    for off in range(1, groups):
        for i, ref in enumerate((pool_ref, lg_ref)):
            copy = pltpu.make_async_remote_copy(
                src_ref=ref.at[group],
                dst_ref=ref.at[group],
                send_sem=group_send.at[off, i],
                recv_sem=group_recv.at[off, i],
                device_id={"group": lax.rem(group + off, groups)},
            )
            copy.start()
            group_copies.append(copy)
    grad_copies = [small(2, grad_mine, pool_grads.at[expert], off) for off in range(1, n)]

    def send_pooled_grad():
        for copy in copies:
            copy.wait()
        pooled_grad = terms[expert]
        for off in range(1, n):
            pooled_grad = pooled_grad + terms_in[off]
        grad_mine[...] = pooled_grad
        pool_grads[pl.ds(expert, 1)] = pooled_grad[None]
        for copy in grad_copies:
            copy.start()
        resid[...] = residual_gradient(resid[...], pooled_grad)

    def pooled_grads_ready():
        for copy in grad_copies:
            copy.wait()

    gather_phase(gbuf, 1, backward_block, [send_pooled_grad, pooled_grads_ready])
    out_ref[...] = (resid[...] + reduce_phase(1)).astype(jnp.bfloat16)
    for copy in group_copies:
        copy.wait()


def body(tokens, w_gate, w_up, w_down, route_ids, route_scores, norm_gain, class_head, targets):
    rows, width = tokens.shape
    n = lax.axis_size("expert")
    groups = lax.axis_size("group")
    local, _, hidden = w_gate.shape
    labels = class_head.shape[1]
    half = n // 2
    gather_weights = w_gate.shape[1] % 16 == 0 and w_down.shape[1] % 16 == 0
    if not gather_weights:
        w_gate = lax.all_gather(w_gate, "group", axis=1, tiled=True)
        w_up = lax.all_gather(w_up, "group", axis=1, tiled=True)
        w_down = lax.all_gather(w_down, "group", axis=1, tiled=True)
    vmem = pl.BlockSpec(memory_space=pltpu.VMEM)
    hbm = pl.BlockSpec(memory_space=pl.ANY)
    dma = pltpu.SemaphoreType.DMA
    bf16, f32 = jnp.bfloat16, jnp.float32
    token_grad, pool, lg = pl.pallas_call(
        functools.partial(kernel, n, groups, gather_weights, n == 8),
        out_shape=(
            jax.ShapeDtypeStruct((rows, width), bf16),
            jax.ShapeDtypeStruct((groups, n, width), f32),
            jax.ShapeDtypeStruct((groups, n, labels), f32),
        ),
        in_specs=[vmem] * 6 + [hbm] * 3,
        out_specs=(vmem, vmem, vmem),
        scratch_shapes=[
            pltpu.VMEM((local, width, hidden), bf16),
            pltpu.VMEM((local, width, hidden), bf16),
            pltpu.VMEM((local, hidden, width), bf16),
            pltpu.VMEM((n, rows, width + LANES), bf16),
            pltpu.VMEM((n, rows, width), bf16),
            pltpu.VMEM((n, local, rows, hidden), f32),
            pltpu.VMEM((n, local, rows, hidden), f32),
            pltpu.VMEM((2, n, rows, width), bf16),
            pltpu.VMEM((2, half, rows, width), bf16),
            pltpu.VMEM((2, half, rows, width), bf16),
            pltpu.VMEM((rows, width), f32),
            pltpu.VMEM((1, width), f32),
            pltpu.VMEM((n, 1, width), f32),
            pltpu.VMEM((n, 1, width), f32),
            pltpu.VMEM((n, 1, width), f32),
            pltpu.VMEM((1, width), f32),
            pltpu.VMEM((n, 1, width), f32),
            dma((3,)),
            dma((groups, 3)),
            dma((groups, 3)),
            dma((2, 4, n)),
            dma((2, 4, n)),
            dma((2, 4, n)),
            dma((2, 4, n)),
            dma((2, 4, n)),
            dma((2, 4, n)),
            dma((2, 4, n)),
            dma((3, n)),
            dma((3, n)),
            dma((groups, 2)),
            dma((groups, 2)),
        ],
        compiler_params=pltpu.CompilerParams(
            collective_id=0, has_side_effects=True, vmem_limit_bytes=60 * 1024 * 1024
        ),
    )(
        tokens,
        route_ids.T,
        route_scores.T,
        norm_gain.reshape(1, width),
        class_head,
        targets,
        w_gate,
        w_up,
        w_down,
    )
    head_grad = lax.dot_general(
        pool.reshape(-1, width).astype(bf16),
        lg.reshape(-1, labels).astype(bf16),
        (((0,), (0,)), ((), ())),
        preferred_element_type=f32,
    )
    return token_grad, head_grad


def solution(mesh):
    in_specs = (
        P(("rep", "expert", "group"), None),
        P("expert", "group", None),
        P("expert", "group", None),
        P("expert", "group", None),
        P(("rep", "expert", "group"), None),
        P(("rep", "expert", "group"), None),
        P(),
        P(None, "expert"),
        P("rep", "group", "expert"),
    )
    out_specs = (P(("rep", "expert", "group"), None), P("rep", "expert"))
    return jax.shard_map(body, mesh=mesh, in_specs=in_specs, out_specs=out_specs, check_vma=False)
```

```python
import functools

import jax
import jax.numpy as jnp
from jax import lax
from jax.experimental import pallas as pl
from jax.experimental.pallas import tpu as pltpu
from jax.sharding import PartitionSpec as P

LOSS_SCALE = 8.0
NORM_EPS = 1e-06
LANES = 128
HALF = 64
NT = (((1,), (1,)), ((), ()))


def ring_place(expert, n, snake):
    if not snake:
        return expert
    odd = lax.rem(expert, 2)
    return (1 - odd) * (expert // 2) + odd * (n - 1 - expert // 2)


def ring_expert(place, n, snake):
    if not snake:
        return place
    back = place // (n // 2)
    return (1 - back) * 2 * place + back * (2 * n - 1 - 2 * place)


def kernel(
    n,
    groups,
    gather_weights,
    snake,
    tok_ref,
    ids_ref,
    score_ref,
    gain_ref,
    head_ref,
    target_ref,
    wg_ref,
    wu_ref,
    wd_ref,
    out_ref,
    pool_ref,
    lg_ref,
    wg,
    wu,
    wd,
    xbuf,
    gbuf,
    gate_coef,
    up_coef,
    part,
    from_right,
    from_left,
    resid,
    pool_mine,
    pool_all,
    terms,
    terms_in,
    grad_mine,
    pool_grads,
    w_local_sem,
    w_send_sem,
    w_recv_sem,
    cw_send,
    ccw_send,
    ring_recv,
    left_send,
    right_send,
    left_recv,
    right_recv,
    small_send,
    small_recv,
    group_send,
    group_recv,
):
    rows, width = tok_ref.shape
    local, _, hidden = wg.shape
    half = n // 2
    expert = lax.axis_index("expert")
    group = lax.axis_index("group")
    place = ring_place(expert, n, snake)
    right = ring_expert(lax.rem(place + 1, n), n, snake)
    left = ring_expert(lax.rem(place + n - 1, n), n, snake)

    barrier = pltpu.get_barrier_semaphore()
    for off in range(1, n):
        pl.semaphore_signal(barrier, inc=1, device_id={"expert": lax.rem(expert + off, n)})
    for off in range(1, groups):
        pl.semaphore_signal(barrier, inc=1, device_id={"group": lax.rem(group + off, groups)})

    locals_ = []
    for i, (src, dst) in enumerate(((wg_ref, wg), (wu_ref, wu), (wd_ref, wd))):
        span = src.shape[1]
        at = pl.multiple_of(group * span, 16) if gather_weights else 0
        copy = pltpu.make_async_copy(src, dst.at[:, pl.ds(at, span), :], w_local_sem.at[i])
        copy.start()
        locals_.append(copy)

    ids = ids_ref[...]
    score = score_ref[...]
    weight = score / jnp.sum(score, axis=0, keepdims=True)
    lane = lax.rem(lax.broadcasted_iota(jnp.int32, (rows, LANES), 1), HALF)
    low = lax.broadcasted_iota(jnp.int32, (rows, LANES), 1) < HALF
    named = lax.rem(lax.broadcasted_iota(jnp.int32, (LANES, rows), 0), HALF)
    by_expert = jnp.zeros((LANES, rows), jnp.float32)
    for k in range(ids.shape[0]):
        by_expert += jnp.where(named == ids[k : k + 1, :], weight[k : k + 1, :], 0.0)
    by_expert = by_expert.T
    high_part = by_expert.astype(jnp.bfloat16).astype(jnp.float32)
    xbuf[0, :, :width] = tok_ref[...]
    xbuf[0, :, width:] = jnp.where(low, high_part, by_expert - high_part).astype(jnp.bfloat16)

    pl.semaphore_wait(barrier, n - 1 + groups - 1)

    pieces = 4
    piece = rows // pieces
    turn = pieces // 2

    def chunk(buf, at, c):
        return buf.at[(*at, pl.ds(c * piece, piece))]

    def cw(buf, phase, k, c):
        return pltpu.make_async_remote_copy(
            src_ref=chunk(buf, (k,), c),
            dst_ref=chunk(buf, (k + 1,), c),
            send_sem=cw_send.at[phase, c, k],
            recv_sem=ring_recv.at[phase, c, k + 1],
            device_id={"expert": right},
        )

    def ccw(buf, phase, k, c):
        return pltpu.make_async_remote_copy(
            src_ref=chunk(buf, (lax.rem(k, n),), c),
            dst_ref=chunk(buf, (k - 1,), c),
            send_sem=ccw_send.at[phase, c, k - 1],
            recv_sem=ring_recv.at[phase, c, k - 1],
            device_id={"expert": left},
        )

    for c in range(pieces):
        cw(xbuf, 0, 0, c).start()
        ccw(xbuf, 0, n, c).start()

    w_copies = []
    if gather_weights:
        for off in range(1, groups):
            for i, (src, dst) in enumerate(((wg_ref, wg), (wu_ref, wu), (wd_ref, wd))):
                span = src.shape[1]
                at = pl.multiple_of(group * span, 16)
                copy = pltpu.make_async_remote_copy(
                    src_ref=src,
                    dst_ref=dst.at[:, pl.ds(at, span), :],
                    send_sem=w_send_sem.at[off, i],
                    recv_sem=w_recv_sem.at[off, i],
                    device_id={"group": lax.rem(group + off, groups)},
                )
                copy.start()
                w_copies.append(copy)

    def weights_ready():
        for copy in locals_:
            copy.wait()
        for copy in w_copies:
            copy.wait()

    def stacked(values):
        return jnp.concatenate(values, axis=0) if len(values) > 1 else values[0]

    def forward_block(slots):
        x = stacked([xbuf[k, :, :width] for k in slots])
        exts = [xbuf[k, :, width:].astype(jnp.float32) for k in slots]
        total = jnp.zeros(x.shape, jnp.float32)
        for j in range(local):
            mine = lane == expert * local + j
            w = stacked([jnp.sum(jnp.where(mine, e, 0.0), axis=1, keepdims=True) for e in exts])
            gate = jnp.dot(x, wg[j], preferred_element_type=jnp.float32)
            up = jnp.dot(x, wu[j], preferred_element_type=jnp.float32)
            sig = 1.0 / (1.0 + jnp.exp(-gate))
            silu = gate * sig * w
            slope = up * (sig * (1.0 + gate * (1.0 - sig))) * w
            for at, k in enumerate(slots):
                gate_coef[k, j] = slope[at * rows : (at + 1) * rows]
                up_coef[k, j] = silu[at * rows : (at + 1) * rows]
            total += jnp.dot(
                (silu * up).astype(jnp.bfloat16), wd[j], preferred_element_type=jnp.float32
            )
        for at, k in enumerate(slots):
            part[0, k] = total[at * rows : (at + 1) * rows].astype(jnp.bfloat16)

    def residual_gradient(residual, pooled_grad):
        inv_rms = lax.rsqrt(jnp.mean(residual * residual, axis=-1, keepdims=True) + NORM_EPS)
        scaled = gain_ref[...] * pooled_grad / rows
        cube = inv_rms * inv_rms * inv_rms
        return inv_rms * scaled - residual * (
            cube * jnp.mean(residual * scaled, axis=-1, keepdims=True)
        )

    def backward_block(slots):
        grads = []
        for k in slots:
            source = ring_expert(lax.rem(place - k + n, n), n, snake)
            grad = residual_gradient(gbuf[k].astype(jnp.float32), pool_grads[source])
            grads.append(grad.astype(jnp.bfloat16))
        g = stacked(grads)
        total = jnp.zeros(g.shape, jnp.float32)
        for j in range(local):
            back = lax.dot_general(g, wd[j], NT, preferred_element_type=jnp.float32)
            gate_grad = (back * stacked([gate_coef[k, j] for k in slots])).astype(jnp.bfloat16)
            up_grad = (back * stacked([up_coef[k, j] for k in slots])).astype(jnp.bfloat16)
            total += lax.dot_general(gate_grad, wg[j], NT, preferred_element_type=jnp.float32)
            total += lax.dot_general(up_grad, wu[j], NT, preferred_element_type=jnp.float32)
        for at, k in enumerate(slots):
            part[1, k] = total[at * rows : (at + 1) * rows].astype(jnp.bfloat16)

    def gather_phase(buf, phase, block, ready):
        def arrive(s):
            for c in range(pieces):
                cw(buf, phase, s - 1, c).wait_recv()

                @pl.when((s < half - 1) | (c < turn))
                def _():
                    cw(buf, phase, s, c).start()

                ccw(buf, phase, n - s + 1, c).wait_recv()

                @pl.when((s < half - 1) | (c >= turn))
                def _():
                    ccw(buf, phase, n - s, c).start()

        lead = len(ready) - 1
        for at, action in enumerate(ready):
            arrive(jnp.int32(at + 1))
            action()

        block((0,))

        def step(s, carry):
            @pl.when((s > 1) & (s + lead < half))
            def _():
                arrive(s + lead)

            block((s, n - s))
            return carry

        lax.fori_loop(1, half, step, 0)
        for c in range(turn):
            to_right(phase, half - 1, c).start()
            to_left(phase, half - 1, c + turn).start()
        for c in range(turn):
            cw(buf, phase, half - 1, c).wait_recv()
            ccw(buf, phase, half + 1, c + turn).wait_recv()
        block((half,))
        for c in range(pieces):

            def drain_cw(k, carry):
                cw(buf, phase, k, c).wait_send()
                return carry

            def drain_ccw(k, carry):
                ccw(buf, phase, n - k, c).wait_send()
                return carry

            lax.fori_loop(0, half - c // turn, drain_cw, 0)
            lax.fori_loop(0, half - 1 + c // turn, drain_ccw, 0)

    def to_left(phase, k, c):
        return pltpu.make_async_remote_copy(
            src_ref=chunk(part, (phase, k), c),
            dst_ref=chunk(from_right, (phase, k - 1), c),
            send_sem=left_send.at[phase, c, k],
            recv_sem=left_recv.at[phase, c, k - 1],
            device_id={"expert": left},
        )

    def to_right(phase, d, c):
        return pltpu.make_async_remote_copy(
            src_ref=chunk(part, (phase, n - d), c),
            dst_ref=chunk(from_left, (phase, d - 1), c),
            send_sem=right_send.at[phase, c, d],
            recv_sem=right_recv.at[phase, c, d - 1],
            device_id={"expert": right},
        )

    def add_piece(phase, slot, incoming, at, c):
        span = pl.ds(c * piece, piece)
        part[phase, slot, span] = (
            part[phase, slot, span].astype(jnp.float32)
            + incoming[phase, at, span].astype(jnp.float32)
        ).astype(jnp.bfloat16)

    def reduce_phase(phase):
        for c in range(turn):
            to_left(phase, half, c).start()
            to_right(phase, half, c + turn).start()

        def pass_left(k, c):
            to_left(phase, k + 1, c).wait_recv()
            add_piece(phase, k, from_right, k, c)
            to_left(phase, k, c).start()

        def pass_right(d, c):
            to_right(phase, d + 1, c).wait_recv()
            add_piece(phase, n - d, from_left, d, c)
            to_right(phase, d, c).start()

        def step(s, carry):
            for c in range(turn):
                pass_left(half - s, c)
                pass_right(half - s, c + turn)

            @pl.when(s < half - 1)
            def _():
                for c in range(turn):
                    pass_right(half - 1 - s, c)
                    pass_left(half - 1 - s, c + turn)

            return carry

        lax.fori_loop(1, half, step, 0)
        for c in range(pieces):
            to_right(phase, 1, c).wait_recv()
            to_left(phase, 1, c).wait_recv()

            def drain_left(k, carry):
                to_left(phase, k, c).wait_send()
                return carry

            def drain_right(d, carry):
                to_right(phase, d, c).wait_send()
                return carry

            lax.fori_loop(1, half + 1 - c // turn, drain_left, 0)
            lax.fori_loop(1, half + c // turn, drain_right, 0)
        return (
            part[phase, 0].astype(jnp.float32)
            + from_right[phase, 0].astype(jnp.float32)
            + from_left[phase, 0].astype(jnp.float32)
        )

    gather_phase(xbuf, 0, forward_block, [weights_ready])
    residual = xbuf[0, :, :width].astype(jnp.float32) + reduce_phase(0)
    gain = gain_ref[...]
    inv_rms = lax.rsqrt(jnp.mean(residual * residual, axis=-1, keepdims=True) + NORM_EPS)
    resid[...] = residual
    gbuf[0] = residual.astype(jnp.bfloat16)
    pooled = jnp.sum(residual * inv_rms * gain, axis=0, keepdims=True) / rows
    pooled = pooled.astype(jnp.bfloat16).astype(jnp.float32)
    pool_mine[...] = pooled
    pool_all[pl.ds(expert, 1)] = pooled[None]

    def small(i, src, dst, off):
        return pltpu.make_async_remote_copy(
            src_ref=src,
            dst_ref=dst,
            send_sem=small_send.at[i, off],
            recv_sem=small_recv.at[i, off],
            device_id={"expert": lax.rem(expert + off, n)},
        )

    copies = [small(0, pool_mine, pool_all.at[expert], off) for off in range(1, n)]
    for copy in copies:
        copy.start()
    for c in range(pieces):
        cw(gbuf, 1, 0, c).start()
        ccw(gbuf, 1, n, c).start()
    for copy in copies:
        copy.wait()
    pooled_rows = jnp.concatenate([pool_all[i] for i in range(n)], axis=0).astype(jnp.bfloat16)
    logits = jnp.dot(pooled_rows, head_ref[...], preferred_element_type=jnp.float32)
    target_rows = jnp.concatenate([target_ref[i] for i in range(n)], axis=0)
    sig = 1.0 / (1.0 + jnp.exp(-logits))
    logit_grad = (LOSS_SCALE * (sig - target_rows.astype(jnp.float32))).astype(jnp.bfloat16)
    pooled_terms = lax.dot_general(logit_grad, head_ref[...], NT, preferred_element_type=jnp.float32)
    for i in range(n):
        terms[i] = pooled_terms[i : i + 1, :]
    copies = [
        small(1, terms.at[lax.rem(expert + off, n)], terms_in.at[off], off) for off in range(1, n)
    ]
    for copy in copies:
        copy.start()
    pool_ref[pl.ds(group, 1)] = pooled_rows.astype(jnp.float32)[None]
    lg_ref[pl.ds(group, 1)] = logit_grad.astype(jnp.float32)[None]
    group_copies = []
    for off in range(1, groups):
        for i, ref in enumerate((pool_ref, lg_ref)):
            copy = pltpu.make_async_remote_copy(
                src_ref=ref.at[group],
                dst_ref=ref.at[group],
                send_sem=group_send.at[off, i],
                recv_sem=group_recv.at[off, i],
                device_id={"group": lax.rem(group + off, groups)},
            )
            copy.start()
            group_copies.append(copy)
    grad_copies = [small(2, grad_mine, pool_grads.at[expert], off) for off in range(1, n)]

    def send_pooled_grad():
        for copy in copies:
            copy.wait()
        pooled_grad = terms[expert]
        for off in range(1, n):
            pooled_grad = pooled_grad + terms_in[off]
        grad_mine[...] = pooled_grad
        pool_grads[pl.ds(expert, 1)] = pooled_grad[None]
        for copy in grad_copies:
            copy.start()
        resid[...] = residual_gradient(resid[...], pooled_grad)

    def pooled_grads_ready():
        for copy in grad_copies:
            copy.wait()

    gather_phase(gbuf, 1, backward_block, [send_pooled_grad, pooled_grads_ready])
    out_ref[...] = (resid[...] + reduce_phase(1)).astype(jnp.bfloat16)
    for copy in group_copies:
        copy.wait()


def body(tokens, w_gate, w_up, w_down, route_ids, route_scores, norm_gain, class_head, targets):
    rows, width = tokens.shape
    n = lax.axis_size("expert")
    groups = lax.axis_size("group")
    local, _, hidden = w_gate.shape
    labels = class_head.shape[1]
    half = n // 2
    gather_weights = w_gate.shape[1] % 16 == 0 and w_down.shape[1] % 16 == 0
    if not gather_weights:
        w_gate = lax.all_gather(w_gate, "group", axis=1, tiled=True)
        w_up = lax.all_gather(w_up, "group", axis=1, tiled=True)
        w_down = lax.all_gather(w_down, "group", axis=1, tiled=True)
    vmem = pl.BlockSpec(memory_space=pltpu.VMEM)
    hbm = pl.BlockSpec(memory_space=pl.ANY)
    dma = pltpu.SemaphoreType.DMA
    bf16, f32 = jnp.bfloat16, jnp.float32
    token_grad, pool, lg = pl.pallas_call(
        functools.partial(kernel, n, groups, gather_weights, n == 8),
        out_shape=(
            jax.ShapeDtypeStruct((rows, width), bf16),
            jax.ShapeDtypeStruct((groups, n, width), f32),
            jax.ShapeDtypeStruct((groups, n, labels), f32),
        ),
        in_specs=[vmem] * 6 + [hbm] * 3,
        out_specs=(vmem, vmem, vmem),
        scratch_shapes=[
            pltpu.VMEM((local, width, hidden), bf16),
            pltpu.VMEM((local, width, hidden), bf16),
            pltpu.VMEM((local, hidden, width), bf16),
            pltpu.VMEM((n, rows, width + LANES), bf16),
            pltpu.VMEM((n, rows, width), bf16),
            pltpu.VMEM((n, local, rows, hidden), f32),
            pltpu.VMEM((n, local, rows, hidden), f32),
            pltpu.VMEM((2, n, rows, width), bf16),
            pltpu.VMEM((2, half, rows, width), bf16),
            pltpu.VMEM((2, half, rows, width), bf16),
            pltpu.VMEM((rows, width), f32),
            pltpu.VMEM((1, width), f32),
            pltpu.VMEM((n, 1, width), f32),
            pltpu.VMEM((n, 1, width), f32),
            pltpu.VMEM((n, 1, width), f32),
            pltpu.VMEM((1, width), f32),
            pltpu.VMEM((n, 1, width), f32),
            dma((3,)),
            dma((groups, 3)),
            dma((groups, 3)),
            dma((2, 4, n)),
            dma((2, 4, n)),
            dma((2, 4, n)),
            dma((2, 4, n)),
            dma((2, 4, n)),
            dma((2, 4, n)),
            dma((2, 4, n)),
            dma((3, n)),
            dma((3, n)),
            dma((groups, 2)),
            dma((groups, 2)),
        ],
        compiler_params=pltpu.CompilerParams(
            collective_id=0, has_side_effects=True, vmem_limit_bytes=60 * 1024 * 1024
        ),
    )(
        tokens,
        route_ids.T,
        route_scores.T,
        norm_gain.reshape(1, width),
        class_head,
        targets,
        w_gate,
        w_up,
        w_down,
    )
    head_grad = lax.dot_general(
        pool.reshape(-1, width).astype(bf16),
        lg.reshape(-1, labels).astype(bf16),
        (((0,), (0,)), ((), ())),
        preferred_element_type=f32,
    )
    return token_grad, head_grad


def solution(mesh):
    in_specs = (
        P(("rep", "expert", "group"), None),
        P("expert", "group", None),
        P("expert", "group", None),
        P("expert", "group", None),
        P(("rep", "expert", "group"), None),
        P(("rep", "expert", "group"), None),
        P(),
        P(None, "expert"),
        P("rep", "group", "expert"),
    )
    out_specs = (P(("rep", "expert", "group"), None), P("rep", "expert"))
    return jax.shard_map(body, mesh=mesh, in_specs=in_specs, out_specs=out_specs, check_vma=False)
```
